512 devices in a mesh: blk: 64 (over y, z_lo, core), head: 8 (over z_hi, x).
Axes of the slice: x: 4, y: 8, z: 8 (z_hi: 2, z_lo: 4; z = z_hi * 4 + z_lo), core: 2. Of those that a mesh axis runs over, the one named last changes fastest.
Arguments:
- queries: bfloat16 [512, 8192], P('blk', 'head'), may hold values from -16 to 16
- keys: bfloat16 [131072, 1024], P('blk', 'head'), may hold values from -16 to 16
- values: bfloat16 [131072, 1024], P('blk', 'head'), may hold values from -24 to 24
- cutoffs: int32 [512], P('blk'), may hold values from 2 to 131072
- out_weight: bfloat16 [8192, 8192], P('head', 'blk'), may hold values from -0.0625 to 0.0625
Outputs:
- projected: float32 [512, 8192], P('head', 'blk')
The draws below stay inside these ranges and needn't reach their ends.
All inputs are finite; a program needn't handle non-finite values.
Results may differ from the reference program's by a relative error of at most 0.0045.
Values may be sent and summed in bfloat16 or wider, within the bound.
No kernel may reach another device: no remote copies, remote signals or barrier semaphores. Data moves between devices by JAX's collectives and lax.ppermute only.
A program may use at most 128 MiB of HBM per device.

```python
import jax
import jax.numpy as jnp
from jax import lax

D = 8192
HEADS = 64
KV_HEADS = 8
HEAD_DIM = 128
KV_DEV = 2048
GROUP = 8
NK = 131072
ROWS = 512
N_BLK = 64


def draw_queries(key, part):
    key = jax.random.fold_in(key, 11)
    first = jax.random.fold_in(key, 0)
    base = jax.random.normal(first, (ROWS, HEADS * HEAD_DIM), jnp.float32)
    return jnp.clip(base, -6.0, 6.0).astype(jnp.bfloat16)


def draw_keys(key, part):
    key = jax.random.fold_in(key, 12)
    first = jax.random.fold_in(key, 0)
    base = jax.random.normal(first, (NK, KV_HEADS * HEAD_DIM), jnp.float32)
    return jnp.clip(base, -6.0, 6.0).astype(jnp.bfloat16)


def draw_values(key, part):
    key = jax.random.fold_in(key, 13)
    first, second = jax.random.split(key)
    offsets = 2.0 * jnp.clip(jax.random.normal(second, (N_BLK, KV_HEADS * HEAD_DIM), jnp.float32), -4.0, 4.0)
    base = jnp.clip(jax.random.normal(first, (NK, KV_HEADS * HEAD_DIM), jnp.float32), -6.0, 6.0)
    return (base + jnp.repeat(offsets, KV_DEV, axis=0)).astype(jnp.bfloat16)


def draw_cutoffs(key, part):
    key = jax.random.fold_in(key, 14)
    first, second = jax.random.split(key)
    one = jax.random.randint(first, (ROWS,), 2, NK + 1, jnp.int32)
    two = jax.random.randint(second, (ROWS,), 2, NK + 1, jnp.int32)
    return jnp.minimum(one, two).at[0].set(NK)


def block_levels(stream_key, shape, pieces, smallest, largest):
    gain = 1.0
    for position, shards_of in pieces:
        steps = jax.random.uniform(jax.random.fold_in(jax.random.fold_in(stream_key, 6), position), (shards_of,), jnp.float32, smallest / len(pieces), largest / len(pieces))
        gain = gain * jnp.repeat(jnp.exp(steps), shape[position] // shards_of).reshape((-1,) + (1,) * (len(shape) - 1 - position))
    return gain


def scatter_about(own_key, shape, deviation, most, pieces=(), kind=jnp.bfloat16):
    drawn = deviation * jax.random.normal(own_key, shape, jnp.float32)
    if pieces:
        drawn = drawn * block_levels(own_key, shape, pieces, -0.22, 0.18)
    return jnp.clip(drawn, -most, most).astype(kind)


def setup_inputs(seed: int = 0) -> dict:
    seeds = jax.random.split(jax.random.key(seed), 6)
    queries = draw_queries(jax.random.fold_in(seeds[5], 71), 0)
    keys = draw_keys(jax.random.fold_in(seeds[5], 71), 0)
    values = draw_values(jax.random.fold_in(seeds[5], 71), 0)
    cutoffs = draw_cutoffs(jax.random.fold_in(seeds[5], 71), 0)
    out_weight = scatter_about(seeds[4], (HEADS * HEAD_DIM, D), (HEADS * HEAD_DIM) ** -0.5, 0.0625, ((0, 8), (1, 64)))
    return dict(queries=queries, keys=keys, values=values, cutoffs=cutoffs, out_weight=out_weight)


NEG = -1e30


def reference(queries, keys, values, cutoffs, out_weight):
    rows = queries.shape[0]
    scale = HEAD_DIM ** -0.5
    q_all = queries.reshape(rows, KV_HEADS, GROUP, HEAD_DIM).transpose(1, 0, 2, 3)
    k_all = keys.reshape(N_BLK, KV_DEV, KV_HEADS, HEAD_DIM).transpose(2, 0, 1, 3)
    v_all = values.reshape(N_BLK, KV_DEV, KV_HEADS, HEAD_DIM).transpose(2, 0, 1, 3)
    starts = jnp.arange(N_BLK, dtype=jnp.int32) * KV_DEV

    def one_head(item):
        q_head, k_head, v_head = item
        q_float = q_head.astype(jnp.float32)

        def visit(carry, block):
            m_old, total, acc = carry
            k_block, v_block, start = block
            scores = jnp.einsum("rgd,kd->rgk", q_float, k_block.astype(jnp.float32)) * scale
            places = start + jnp.arange(KV_DEV, dtype=jnp.int32)
            seen = (places[None, :] < cutoffs[:, None])[:, None, :]
            scores = jnp.where(seen, scores, NEG)
            m_new = jnp.maximum(m_old, jnp.max(scores, axis=-1))
            weights = jnp.where(seen, jnp.exp(scores - m_new[..., None]), 0.0)
            fade = jnp.exp(m_old - m_new)
            total = total * fade + jnp.sum(weights, axis=-1)
            rounded = lax.optimization_barrier(weights.astype(jnp.bfloat16)).astype(jnp.float32)
            acc = acc * fade[..., None] + jnp.einsum("rgk,kd->rgd", rounded, v_block.astype(jnp.float32))
            return (m_new, total, acc), None

        init = (jnp.full((rows, GROUP), NEG, jnp.float32), jnp.zeros((rows, GROUP), jnp.float32),
                jnp.zeros((rows, GROUP, HEAD_DIM), jnp.float32))
        (m_last, total, acc), unused = lax.scan(visit, init, (k_head, v_head, starts))
        return acc / total[..., None]

    mixed = lax.map(one_head, (q_all, k_all, v_all))
    attended = mixed.transpose(1, 0, 2, 3).reshape(rows, HEADS * HEAD_DIM).astype(jnp.bfloat16)
    return jnp.dot(attended, out_weight, preferred_element_type=jnp.float32)
```

```python
import functools
import math

import jax
import jax.numpy as jnp
from jax import lax
from jax.experimental import pallas as pl
from jax.experimental.pallas import tpu as pltpu
from jax.sharding import Mesh
from jax.sharding import PartitionSpec as P

HEAD_DIM = 128
GROUP = 8
LANES = 128
WIDTH = GROUP * HEAD_DIM
PACKED = WIDTH + LANES
NEG = -1e30
FLOOR = -1e20
SCALE = math.log2(math.e) / math.sqrt(HEAD_DIM)
ROW_BLOCK = 32
KEY_CHUNK = 2048
VMEM = 32 * 2**20

AXES = ("y", "z", "c", "w", "x")
SIZES = (8, 4, 2, 2, 4)
BLK = ("y", "z", "c")
HEAD = ("w", "x")
CHIPS = ("y", "z")
SWAP = ((0, 1), (1, 0))


def attend_kernel(q_ref, k_mine, v_mine, k_other, v_other, o_ref):
    length = k_mine.shape[0]
    rows = q_ref.shape[0]
    many = GROUP * rows
    me = lax.axis_index("y") * 4 + lax.axis_index("z")
    core = lax.axis_index("c")
    start_mine = (me * 2 + core) * length
    start_other = (me * 2 + 1 - core) * length
    packed = q_ref[...]
    queries = jnp.concatenate(
        [packed[:, h * HEAD_DIM : (h + 1) * HEAD_DIM] for h in range(GROUP)], axis=0
    )
    digits = packed[:, WIDTH:].astype(jnp.float32)
    cut = (digits[:, 0:1] + 64.0 * digits[:, 1:2] + 4096.0 * digits[:, 2:3]).astype(jnp.int32)
    cut = jnp.concatenate([cut] * GROUP, axis=0)
    places = lax.broadcasted_iota(jnp.int32, (many, KEY_CHUNK), 1)
    ones = jnp.ones((KEY_CHUNK, LANES), jnp.bfloat16)
    chunks = [
        (keys, values, start + at, at)
        for keys, values, start in (
            (k_mine, v_mine, start_mine),
            (k_other, v_other, start_other),
        )
        for at in range(0, length, KEY_CHUNK)
    ]

    def scores_of(chunk):
        keys, _, start, at = chunk
        scores = lax.dot_general(
            queries,
            keys[at : at + KEY_CHUNK, :],
            (((1,), (1,)), ((), ())),
            preferred_element_type=jnp.float32,
        )
        return jnp.where(places < cut - start, scores, NEG)

    m_old = jnp.full((many, 1), FLOOR, jnp.float32)
    acc = jnp.zeros((many, HEAD_DIM + LANES), jnp.float32)
    scores = scores_of(chunks[0])
    for n, (_, values, _, at) in enumerate(chunks):
        later = scores_of(chunks[n + 1]) if n + 1 < len(chunks) else None
        m_new = jnp.maximum(m_old, jnp.max(scores, axis=1, keepdims=True))
        fade = jnp.exp2((m_old - m_new) * SCALE)
        weights = jnp.exp2(scores * SCALE - m_new * SCALE).astype(jnp.bfloat16)
        wide = jnp.concatenate([values[at : at + KEY_CHUNK, :], ones], axis=1)
        acc = acc * fade + jnp.dot(weights, wide, preferred_element_type=jnp.float32)
        m_old, scores = m_new, later
    total = acc[:, HEAD_DIM : HEAD_DIM + 1]
    some = jnp.maximum(total, 1e-30)
    mixed = (acc[:, :HEAD_DIM] / some).astype(jnp.bfloat16)
    level = jnp.where(total > 0.0, m_old * SCALE + jnp.log2(some), NEG)
    high = level.astype(jnp.bfloat16).astype(jnp.float32)
    middle = (level - high).astype(jnp.bfloat16).astype(jnp.float32)
    low = (level - high) - middle
    lane = lax.broadcasted_iota(jnp.int32, (rows, LANES), 1)
    stats = jnp.zeros((rows, LANES), jnp.float32)
    for h in range(GROUP):
        mine = slice(h * rows, (h + 1) * rows)
        o_ref[:, h * HEAD_DIM : (h + 1) * HEAD_DIM] = mixed[mine]
        for i, part in enumerate((high, middle, low)):
            stats = jnp.where(lane == 3 * h + i, part[mine], stats)
    o_ref[:, WIDTH:] = stats.astype(jnp.bfloat16)


def attend(packed, k_mine, v_mine, k_other, v_other):
    rows = packed.shape[0]
    whole = pl.BlockSpec(k_mine.shape, lambda i: (0, 0))
    block = pl.BlockSpec((ROW_BLOCK, PACKED), lambda i: (i, 0))
    return pl.pallas_call(
        attend_kernel,
        grid=(rows // ROW_BLOCK,),
        in_specs=[block, whole, whole, whole, whole],
        out_specs=block,
        out_shape=jax.ShapeDtypeStruct((rows, PACKED), jnp.bfloat16),
        compiler_params=pltpu.CompilerParams(vmem_limit_bytes=VMEM),
        name="attend",
    )(packed, k_mine, v_mine, k_other, v_other)


def repeated(o_ref, at, block):
    twice = jnp.concatenate([block, block], axis=0)
    for top in range(0, o_ref.shape[0], twice.shape[0]):
        o_ref[top : top + twice.shape[0], at : at + block.shape[1]] = twice


def pack_kernel(q_ref, cut_ref, o_ref):
    rows = q_ref.shape[0]
    lane = lax.broadcasted_iota(jnp.int32, (rows, LANES), 1)
    row = lax.broadcasted_iota(jnp.int32, (rows, LANES), 0)
    cut = jnp.zeros((rows, LANES), jnp.int32)
    for r in range(rows):
        cut = jnp.where(row == r, cut_ref[r], cut)
    digits = jnp.where(lane == 0, cut & 63, jnp.where(lane == 1, (cut >> 6) & 63, cut >> 12))
    digits = digits.astype(jnp.float32).astype(jnp.bfloat16)
    repeated(o_ref, 0, q_ref[...])
    repeated(o_ref, WIDTH, digits)


def pack(queries, cutoffs, receivers):
    rows = queries.shape[0]
    return pl.pallas_call(
        pack_kernel,
        in_specs=[
            pl.BlockSpec(memory_space=pltpu.VMEM),
            pl.BlockSpec(memory_space=pltpu.SMEM),
        ],
        out_shape=jax.ShapeDtypeStruct((receivers * rows, PACKED), jnp.bfloat16),
        name="pack",
    )(queries, cutoffs)


def combine_kernel(p_ref, o_ref):
    rows = 8
    sources = p_ref.shape[0] // rows
    levels = []
    for n in range(sources // 2):
        stats = p_ref[2 * n * rows : 2 * (n + 1) * rows, WIDTH:].astype(jnp.float32)
        level = stats + jnp.roll(stats, -1, axis=1) + jnp.roll(stats, -2, axis=1)
        levels += [level[:rows], level[rows:]]
    top = functools.reduce(jnp.maximum, levels)
    shares = [jnp.exp2(level - top) for level in levels]
    total = 1.0 / functools.reduce(jnp.add, shares)
    shares = [share * total for share in shares]
    sums = [jnp.zeros((rows, HEAD_DIM), jnp.float32) for _ in range(GROUP)]
    for n in range(sources // 2):
        for h in range(GROUP):
            part = p_ref[2 * n * rows : 2 * (n + 1) * rows, h * HEAD_DIM : (h + 1) * HEAD_DIM]
            part = part.astype(jnp.float32)
            sums[h] = sums[h] + part[:rows] * shares[2 * n][:, 3 * h : 3 * h + 1]
            sums[h] = sums[h] + part[rows:] * shares[2 * n + 1][:, 3 * h : 3 * h + 1]
    for h in range(GROUP):
        repeated(o_ref, h * HEAD_DIM, sums[h].astype(jnp.bfloat16))


def combine(parts):
    return pl.pallas_call(
        combine_kernel,
        out_shape=jax.ShapeDtypeStruct((parts.shape[0], WIDTH), jnp.bfloat16),
        name="combine",
    )(parts)


def project_kernel(a_ref, w_mine, w_other, o_ref):
    rows = a_ref.shape[0]
    core = lax.axis_index("c")
    attended = a_ref[...]
    for place, weight in ((core, w_mine), (1 - core, w_other)):
        at = pl.multiple_of(place * rows, rows)
        o_ref[pl.ds(at, rows), :] = jnp.dot(
            attended, weight[...], preferred_element_type=jnp.float32
        )


def project(attended, w_mine, w_other):
    rows = attended.shape[0]
    return pl.pallas_call(
        project_kernel,
        out_shape=jax.ShapeDtypeStruct((2 * rows, w_mine.shape[1]), jnp.float32),
        name="project",
    )(attended, w_mine, w_other)


def exchange(x, axis):
    return lax.all_to_all(x, axis, 0, 0, tiled=True)


def shards(queries, keys, values, cutoffs, out_weight):
    rows = queries.shape[0]
    chips = SIZES[0] * SIZES[1]
    k_other = lax.ppermute(keys, "c", SWAP)
    v_other = lax.ppermute(values, "c", SWAP)
    w_other = lax.ppermute(out_weight, "c", SWAP)
    packed = exchange(pack(queries, cutoffs, chips), CHIPS)
    parts = exchange(attend(packed, keys, values, k_other, v_other), CHIPS)
    attended = exchange(combine(parts), CHIPS)
    sums = exchange(project(attended, out_weight, w_other), ("c",) + HEAD)
    heads = SIZES[3] * SIZES[4]
    sums = sums.reshape(2, heads, SIZES[1], rows, LANES).sum(axis=1)
    return sums.transpose(1, 0, 2, 3).reshape(2 * SIZES[1] * rows, LANES)


def solution(mesh):
    fine = Mesh(mesh.devices.reshape(SIZES), AXES)
    return jax.shard_map(
        shards,
        mesh=fine,
        in_specs=(P(BLK, HEAD), P(BLK, HEAD), P(BLK, HEAD), P(BLK), P(HEAD, BLK)),
        out_specs=P(HEAD, BLK),
        check_vma=False,
    )
```

```python
import functools
import math

import jax
import jax.numpy as jnp
from jax import lax
from jax.experimental import pallas as pl
from jax.experimental.pallas import tpu as pltpu
from jax.sharding import Mesh
from jax.sharding import PartitionSpec as P

HEAD_DIM = 128
GROUP = 8
LANES = 128
WIDTH = GROUP * HEAD_DIM
PACKED = WIDTH + LANES
NEG = -1e30
FLOOR = -1e20
SCALE = math.log2(math.e) / math.sqrt(HEAD_DIM)
ROW_BLOCK = 32
KEY_CHUNK = 2048
VMEM = 24 * 2**20
SMALL = 8 * 2**20

AXES = ("y", "zh", "zl", "c", "w", "x")
SIZES = (8, 2, 2, 2, 2, 4)
BLK = ("y", "zh", "zl", "c")
HEAD = ("w", "x")
CHIPS = ("y", "zh", "zl")
FAR = ("y", "zh")
NEAR = ("zl", "c")
SWAP = ((0, 1), (1, 0))


def attend_kernel(q_ref, k_mine, v_mine, k_other, v_other, o_ref):
    length = k_mine.shape[0]
    rows = q_ref.shape[0]
    many = GROUP * rows
    me = lax.axis_index("y") * 4 + lax.axis_index("zh") * 2 + lax.axis_index("zl")
    core = lax.axis_index("c")
    start_mine = (me * 2 + core) * length
    start_other = (me * 2 + 1 - core) * length
    packed = q_ref[...]
    queries = jnp.concatenate(
        [packed[:, h * HEAD_DIM : (h + 1) * HEAD_DIM] for h in range(GROUP)], axis=0
    )
    digits = packed[:, WIDTH:].astype(jnp.float32)
    cut = (digits[:, 0:1] + 64.0 * digits[:, 1:2] + 4096.0 * digits[:, 2:3]).astype(jnp.int32)
    cut = jnp.concatenate([cut] * GROUP, axis=0)
    places = lax.broadcasted_iota(jnp.int32, (many, KEY_CHUNK), 1)
    ones = jnp.ones((KEY_CHUNK, LANES), jnp.bfloat16)
    chunks = [
        (keys, values, start + at, at)
        for keys, values, start in (
            (k_mine, v_mine, start_mine),
            (k_other, v_other, start_other),
        )
        for at in range(0, length, KEY_CHUNK)
    ]

    def scores_of(chunk):
        keys, _, start, at = chunk
        scores = lax.dot_general(
            queries,
            keys[at : at + KEY_CHUNK, :],
            (((1,), (1,)), ((), ())),
            preferred_element_type=jnp.float32,
        )
        return jnp.where(places < cut - start, scores, NEG)

    m_old = jnp.full((many, 1), FLOOR, jnp.float32)
    acc = jnp.zeros((many, HEAD_DIM + LANES), jnp.float32)
    scores = scores_of(chunks[0])
    for n, (_, values, _, at) in enumerate(chunks):
        later = scores_of(chunks[n + 1]) if n + 1 < len(chunks) else None
        m_new = jnp.maximum(m_old, jnp.max(scores, axis=1, keepdims=True))
        fade = jnp.exp2((m_old - m_new) * SCALE)
        weights = jnp.exp2(scores * SCALE - m_new * SCALE).astype(jnp.bfloat16)
        wide = jnp.concatenate([values[at : at + KEY_CHUNK, :], ones], axis=1)
        acc = acc * fade + jnp.dot(weights, wide, preferred_element_type=jnp.float32)
        m_old, scores = m_new, later
    total = acc[:, HEAD_DIM : HEAD_DIM + 1]
    some = jnp.maximum(total, 1e-30)
    mixed = (acc[:, :HEAD_DIM] / some).astype(jnp.bfloat16)
    level = jnp.where(total > 0.0, m_old * SCALE + jnp.log2(some), NEG)
    high = level.astype(jnp.bfloat16).astype(jnp.float32)
    middle = (level - high).astype(jnp.bfloat16).astype(jnp.float32)
    low = (level - high) - middle
    lane = lax.broadcasted_iota(jnp.int32, (rows, LANES), 1)
    stats = jnp.zeros((rows, LANES), jnp.float32)
    for h in range(GROUP):
        mine = slice(h * rows, (h + 1) * rows)
        o_ref[:, h * HEAD_DIM : (h + 1) * HEAD_DIM] = mixed[mine]
        for i, part in enumerate((high, middle, low)):
            stats = jnp.where(lane == 3 * h + i, part[mine], stats)
    o_ref[:, WIDTH:] = stats.astype(jnp.bfloat16)


def attend(packed, k_mine, v_mine, k_other, v_other):
    rows = packed.shape[0]
    whole = pl.BlockSpec(k_mine.shape, lambda i: (0, 0))
    block = pl.BlockSpec((ROW_BLOCK, PACKED), lambda i: (i, 0))
    return pl.pallas_call(
        attend_kernel,
        grid=(rows // ROW_BLOCK,),
        in_specs=[block, whole, whole, whole, whole],
        out_specs=block,
        out_shape=jax.ShapeDtypeStruct((rows, PACKED), jnp.bfloat16),
        compiler_params=pltpu.CompilerParams(vmem_limit_bytes=VMEM),
        name="attend",
    )(packed, k_mine, v_mine, k_other, v_other)


def repeated(o_ref, at, block):
    twice = jnp.concatenate([block, block], axis=0)
    for top in range(0, o_ref.shape[0], twice.shape[0]):
        o_ref[top : top + twice.shape[0], at : at + block.shape[1]] = twice


def pack_kernel(q_ref, cut_ref, o_ref):
    rows = q_ref.shape[0]
    lane = lax.broadcasted_iota(jnp.int32, (rows, LANES), 1)
    row = lax.broadcasted_iota(jnp.int32, (rows, LANES), 0)
    cut = jnp.zeros((rows, LANES), jnp.int32)
    for r in range(rows):
        cut = jnp.where(row == r, cut_ref[r], cut)
    digits = jnp.where(lane == 0, cut & 63, jnp.where(lane == 1, (cut >> 6) & 63, cut >> 12))
    digits = digits.astype(jnp.float32).astype(jnp.bfloat16)
    repeated(o_ref, 0, q_ref[...])
    repeated(o_ref, WIDTH, digits)


def pack(queries, cutoffs, receivers):
    rows = queries.shape[0]
    return pl.pallas_call(
        pack_kernel,
        in_specs=[
            pl.BlockSpec(memory_space=pltpu.VMEM),
            pl.BlockSpec(memory_space=pltpu.SMEM),
        ],
        out_shape=jax.ShapeDtypeStruct((receivers * rows, PACKED), jnp.bfloat16),
        name="pack",
    )(queries, cutoffs)


def combine_kernel(p_ref, o_ref):
    rows = 8
    sources = p_ref.shape[0] // rows
    levels = []
    for n in range(sources // 2):
        stats = p_ref[2 * n * rows : 2 * (n + 1) * rows, WIDTH:].astype(jnp.float32)
        level = stats + jnp.roll(stats, -1, axis=1) + jnp.roll(stats, -2, axis=1)
        levels += [level[:rows], level[rows:]]
    top = functools.reduce(jnp.maximum, levels)
    shares = [jnp.exp2(level - top) for level in levels]
    total = 1.0 / functools.reduce(jnp.add, shares)
    shares = [share * total for share in shares]
    sums = [jnp.zeros((rows, HEAD_DIM), jnp.float32) for _ in range(GROUP)]
    for n in range(sources // 2):
        for h in range(GROUP):
            part = p_ref[2 * n * rows : 2 * (n + 1) * rows, h * HEAD_DIM : (h + 1) * HEAD_DIM]
            part = part.astype(jnp.float32)
            sums[h] = sums[h] + part[:rows] * shares[2 * n][:, 3 * h : 3 * h + 1]
            sums[h] = sums[h] + part[rows:] * shares[2 * n + 1][:, 3 * h : 3 * h + 1]
    for h in range(GROUP):
        repeated(o_ref, h * HEAD_DIM, sums[h].astype(jnp.bfloat16))


def combine(parts, receivers):
    return pl.pallas_call(
        combine_kernel,
        out_shape=jax.ShapeDtypeStruct((8 * receivers, WIDTH), jnp.bfloat16),
        compiler_params=pltpu.CompilerParams(vmem_limit_bytes=SMALL),
        name="combine",
    )(parts)


def project_kernel(a_ref, w_ref, w_core, w_chip, w_both, o_ref):
    rows = a_ref.shape[0]
    chip = lax.axis_index("zl")
    core = lax.axis_index("c")
    attended = a_ref[...]
    for there, that, weight in (
        (chip, core, w_ref),
        (chip, 1 - core, w_core),
        (1 - chip, core, w_chip),
        (1 - chip, 1 - core, w_both),
    ):
        at = pl.multiple_of((there * 2 + that) * rows, rows)
        part = jnp.dot(attended, weight[...], preferred_element_type=jnp.float32)
        o_ref[pl.ds(at, rows), :] = part.astype(o_ref.dtype)


def project(attended, *weights):
    rows = attended.shape[0]
    return pl.pallas_call(
        project_kernel,
        out_shape=jax.ShapeDtypeStruct((len(weights) * rows, LANES), jnp.bfloat16),
        compiler_params=pltpu.CompilerParams(vmem_limit_bytes=SMALL),
        name="project",
    )(attended, *weights)


def total_kernel(s_ref, o_ref):
    near, heads, rows = 4, 8, 16
    half = rows // 2
    for n in range(near):
        parts = [
            s_ref[(n * heads + h) * rows : (n * heads + h + 1) * rows, :].astype(jnp.float32)
            for h in range(heads)
        ]
        total = functools.reduce(jnp.add, parts)
        for z in range(2):
            at = (z * near + n) * half
            o_ref[at : at + half, :] = total[z * half : (z + 1) * half]


def total_of(sums):
    return pl.pallas_call(
        total_kernel,
        out_shape=jax.ShapeDtypeStruct((64, LANES), jnp.float32),
        compiler_params=pltpu.CompilerParams(vmem_limit_bytes=SMALL),
        name="total",
    )(sums)


def exchange(x, axis):
    return lax.all_to_all(x, axis, 0, 0, tiled=True)


def shards(queries, keys, values, cutoffs, out_weight):
    chips = SIZES[0] * SIZES[1] * SIZES[2]
    far = SIZES[0] * SIZES[1]
    k_other = lax.ppermute(keys, "c", SWAP)
    v_other = lax.ppermute(values, "c", SWAP)
    w_core = lax.ppermute(out_weight, "c", SWAP)
    w_chip = lax.ppermute(out_weight, "zl", SWAP)
    w_both = lax.ppermute(w_chip, "c", SWAP)
    packed = exchange(pack(queries, cutoffs, chips), CHIPS)
    parts = exchange(attend(packed, keys, values, k_other, v_other), CHIPS)
    attended = exchange(combine(parts, far), FAR)
    sums = project(attended, out_weight, w_core, w_chip, w_both)
    return total_of(exchange(sums, NEAR + HEAD))


def solution(mesh):
    fine = Mesh(mesh.devices.reshape(SIZES), AXES)
    return jax.shard_map(
        shards,
        mesh=fine,
        in_specs=(P(BLK, HEAD), P(BLK, HEAD), P(BLK, HEAD), P(BLK), P(HEAD, BLK)),
        out_specs=P(HEAD, BLK),
        check_vma=False,
    )
```

```python
import functools
import math

import jax
import jax.numpy as jnp
from jax import lax
from jax.experimental import pallas as pl
from jax.experimental.pallas import tpu as pltpu
from jax.sharding import Mesh
from jax.sharding import PartitionSpec as P

HEAD_DIM = 128
GROUP = 8
LANES = 128
WIDTH = GROUP * HEAD_DIM
PACKED = WIDTH + LANES
NEG = -1e30
FLOOR = -1e20
SCALE = math.log2(math.e) / math.sqrt(HEAD_DIM)
ROW_BLOCK = 64
PROBE = 128
LEAP = 400.0
VMEM = 24 * 2**20
SMALL = 8 * 2**20

AXES = ("y", "zh", "zl", "c", "w", "x")
SIZES = (8, 2, 2, 2, 2, 4)
BLK = ("y", "zh", "zl", "c")
HEAD = ("w", "x")
FAR = ("y", "zh")
NEAR = ("zl", "c")
SWAP = ((0, 1), (1, 0))


def split(x):
    high = x.astype(jnp.bfloat16).astype(jnp.float32)
    middle = (x - high).astype(jnp.bfloat16).astype(jnp.float32)
    return high, middle, x - high - middle


def attend_kernel(chunk, whose, q_ref, k_mine, v_mine, k_other, v_other, o_ref):
    pairs = ((k_mine, v_mine), (k_other, v_other))
    rows = o_ref.shape[0]
    many = GROUP * ROW_BLOCK
    length = k_mine.shape[0]
    chip = lax.axis_index("zl")
    core = lax.axis_index("c")
    me = lax.axis_index("y") * 8 + lax.axis_index("zh") * 4 + chip * 2
    starts = ((me + core) * length, (me + 1 - core) * length)
    base = (1 - chip if whose else chip) * rows

    def load(i):
        packed = q_ref[pl.ds(pl.multiple_of(base + i * ROW_BLOCK, ROW_BLOCK), ROW_BLOCK), :]
        queries = jnp.concatenate(
            [packed[:, h * HEAD_DIM : (h + 1) * HEAD_DIM] for h in range(GROUP)], axis=0
        )
        digits = packed[:, WIDTH:].astype(jnp.float32)
        cut = digits[:, 0:1] + 64.0 * digits[:, 1:2] + 4096.0 * digits[:, 2:3]
        cut = jnp.concatenate([cut.astype(jnp.int32)] * GROUP, axis=0)
        return queries, cut

    def scores_of(queries, cut, n, at, size):
        scores = lax.dot_general(
            queries,
            pairs[n][0][at : at + size, :],
            (((1,), (1,)), ((), ())),
            preferred_element_type=jnp.float32,
        )
        places = lax.broadcasted_iota(jnp.int32, (many, size), 1)
        return jnp.where(places < cut - (starts[n] + at), scores, NEG)

    def weighed(acc, scores, level, n, at, size):
        weights = jnp.exp2(scores * SCALE - level * SCALE).astype(jnp.bfloat16)
        wide = [pairs[n][1][at : at + size, :], jnp.ones((size, LANES), jnp.bfloat16)]
        wide = jnp.concatenate(wide, axis=1)
        return acc + jnp.dot(weights, wide, preferred_element_type=jnp.float32)

    def store(i, level, acc):
        level = jnp.broadcast_to(level, (many, LANES))
        here = pl.ds(pl.multiple_of(i * ROW_BLOCK, ROW_BLOCK), ROW_BLOCK)
        total = acc[:, HEAD_DIM:]
        some = jnp.maximum(total, 1e-30)
        mixed = (acc[:, :HEAD_DIM] / some).astype(jnp.bfloat16)
        level = jnp.where(total > 0.0, level * SCALE + jnp.log2(some), NEG)
        high, middle, low = split(level)
        lane = lax.broadcasted_iota(jnp.int32, (ROW_BLOCK, LANES), 1)
        stats = jnp.zeros((ROW_BLOCK, LANES), jnp.float32)
        for h in range(GROUP):
            mine = slice(h * ROW_BLOCK, (h + 1) * ROW_BLOCK)
            o_ref[here, h * HEAD_DIM : (h + 1) * HEAD_DIM] = mixed[mine]
            part = jnp.where(lane < 8, high[mine], jnp.where(lane < 16, middle[mine], low[mine]))
            stats = jnp.where((lane & 7) == h, part, stats)
        o_ref[here, WIDTH:] = jnp.where(lane < 24, stats, 0.0).astype(jnp.bfloat16)

    def quick(i, leap):
        queries, cut = load(i)
        acc = jnp.zeros((many, HEAD_DIM + LANES), jnp.float32)
        level = jnp.full((many, 1), FLOOR, jnp.float32)
        for n in range(len(pairs)):
            probe = scores_of(queries, cut, n, 0, PROBE)
            level = jnp.maximum(level, jnp.max(probe, axis=1, keepdims=True))
        most = jnp.full((many, LANES), FLOOR, jnp.float32)
        for n in range(len(pairs)):
            for at in range(0, length, chunk):
                scores = scores_of(queries, cut, n, at, chunk)
                for t in range(0, chunk, LANES):
                    most = jnp.maximum(most, scores[:, t : t + LANES])
                acc = weighed(acc, scores, level, n, at, chunk)
        store(i, level, acc)
        return jnp.maximum(leap, most - level)

    leap = jnp.full((many, LANES), FLOOR, jnp.float32)
    leap = lax.fori_loop(0, rows // ROW_BLOCK, quick, leap)

    @pl.when(jnp.max(leap) > LEAP)
    def _():
        def exact(i, unused):
            queries, cut = load(i)
            acc = jnp.zeros((many, HEAD_DIM + LANES), jnp.float32)
            level = jnp.full((many, 1), FLOOR, jnp.float32)
            for n in range(len(pairs)):
                scores = scores_of(queries, cut, n, 0, length)
                higher = jnp.maximum(level, jnp.max(scores, axis=1, keepdims=True))
                acc = weighed(acc * jnp.exp2((level - higher) * SCALE), scores, higher, n, 0, length)
                level = higher
            store(i, level, acc)
            return unused

        lax.fori_loop(0, rows // ROW_BLOCK, exact, 0)


def attend(packed, whose, *pairs):
    rows = packed.shape[0] // 2
    vmem = pl.BlockSpec(memory_space=pltpu.VMEM)
    work = 4 * rows * GROUP * pairs[0].shape[0] * HEAD_DIM
    return pl.pallas_call(
        functools.partial(attend_kernel, 256, whose),
        in_specs=[vmem] * (1 + len(pairs)),
        out_specs=vmem,
        out_shape=jax.ShapeDtypeStruct((rows, PACKED), jnp.bfloat16),
        compiler_params=pltpu.CompilerParams(vmem_limit_bytes=VMEM),
        cost_estimate=pl.CostEstimate(
            flops=4 * work, bytes_accessed=2**21, transcendentals=work // 256
        ),
        name="attend",
    )(packed, *pairs)


def level_of(stats):
    stats = stats.astype(jnp.float32)
    return stats + jnp.roll(stats, -8, axis=1) + jnp.roll(stats, -16, axis=1)


def merge_kernel(a_ref, b_ref, o_ref):
    rows = 64
    lane = lax.broadcasted_iota(jnp.int32, (rows, LANES), 1)
    for at in range(0, o_ref.shape[0], rows):
        here = slice(at, at + rows)
        levels = [level_of(ref[here, WIDTH:]) for ref in (a_ref, b_ref)]
        top = jnp.maximum(*levels)
        shares = [jnp.exp2(level - top) for level in levels]
        total = shares[0] + shares[1]
        shares = [share / total for share in shares]
        for h in range(GROUP):
            head = slice(h * HEAD_DIM, (h + 1) * HEAD_DIM)
            mixed = a_ref[here, head].astype(jnp.float32) * shares[0][:, h : h + 1]
            mixed = mixed + b_ref[here, head].astype(jnp.float32) * shares[1][:, h : h + 1]
            o_ref[here, head] = mixed.astype(jnp.bfloat16)
        high, middle, low = split(top + jnp.log2(total))
        stats = jnp.where(
            lane < 8,
            high,
            jnp.where(lane < 16, jnp.roll(middle, 8, axis=1), jnp.roll(low, 16, axis=1)),
        )
        o_ref[here, WIDTH:] = jnp.where(lane < 24, stats, 0.0).astype(jnp.bfloat16)


def merge(a, b):
    return pl.pallas_call(
        merge_kernel,
        out_shape=jax.ShapeDtypeStruct(a.shape, a.dtype),
        compiler_params=pltpu.CompilerParams(vmem_limit_bytes=SMALL),
        name="merge",
    )(a, b)


def repeated(o_ref, at, block):
    twice = jnp.concatenate([block, block], axis=0)
    for top in range(0, o_ref.shape[0], twice.shape[0]):
        o_ref[top : top + twice.shape[0], at : at + block.shape[1]] = twice


def pack_kernel(q_ref, cut_ref, o_ref):
    rows = q_ref.shape[0]
    lane = lax.broadcasted_iota(jnp.int32, (rows, LANES), 1)
    row = lax.broadcasted_iota(jnp.int32, (rows, LANES), 0)
    cut = jnp.zeros((rows, LANES), jnp.int32)
    for r in range(rows):
        cut = jnp.where(row == r, cut_ref[r], cut)
    digits = jnp.where(lane == 0, cut & 63, jnp.where(lane == 1, (cut >> 6) & 63, cut >> 12))
    digits = digits.astype(jnp.float32).astype(jnp.bfloat16)
    repeated(o_ref, 0, q_ref[...])
    repeated(o_ref, WIDTH, digits)


def pack(queries, cutoffs, receivers):
    rows = queries.shape[0]
    return pl.pallas_call(
        pack_kernel,
        in_specs=[
            pl.BlockSpec(memory_space=pltpu.VMEM),
            pl.BlockSpec(memory_space=pltpu.SMEM),
        ],
        out_shape=jax.ShapeDtypeStruct((receivers * rows, PACKED), jnp.bfloat16),
        name="pack",
    )(queries, cutoffs)


def combine_kernel(p_ref, o_ref):
    rows = 8
    sources = p_ref.shape[0] // rows
    levels = []
    for n in range(sources // 2):
        level = level_of(p_ref[2 * n * rows : 2 * (n + 1) * rows, WIDTH:])
        levels += [level[:rows], level[rows:]]
    top = functools.reduce(jnp.maximum, levels)
    shares = [jnp.exp2(level - top) for level in levels]
    total = 1.0 / functools.reduce(jnp.add, shares)
    shares = [share * total for share in shares]
    sums = [jnp.zeros((rows, HEAD_DIM), jnp.float32) for _ in range(GROUP)]
    for n in range(sources // 2):
        for h in range(GROUP):
            part = p_ref[2 * n * rows : 2 * (n + 1) * rows, h * HEAD_DIM : (h + 1) * HEAD_DIM]
            part = part.astype(jnp.float32)
            sums[h] = sums[h] + part[:rows] * shares[2 * n][:, h : h + 1]
            sums[h] = sums[h] + part[rows:] * shares[2 * n + 1][:, h : h + 1]
    for h in range(GROUP):
        repeated(o_ref, h * HEAD_DIM, sums[h].astype(jnp.bfloat16))


def combine(parts, receivers):
    return pl.pallas_call(
        combine_kernel,
        out_shape=jax.ShapeDtypeStruct((8 * receivers, WIDTH), jnp.bfloat16),
        compiler_params=pltpu.CompilerParams(vmem_limit_bytes=SMALL),
        name="combine",
    )(parts)


def project_kernel(a_ref, w_ref, w_core, w_chip, w_both, o_ref):
    rows = a_ref.shape[0]
    chip = lax.axis_index("zl")
    core = lax.axis_index("c")
    attended = a_ref[...]
    for there, that, weight in (
        (chip, core, w_ref),
        (chip, 1 - core, w_core),
        (1 - chip, core, w_chip),
        (1 - chip, 1 - core, w_both),
    ):
        at = pl.multiple_of((there * 2 + that) * rows, rows)
        part = jnp.dot(attended, weight[...], preferred_element_type=jnp.float32)
        o_ref[pl.ds(at, rows), :] = part.astype(o_ref.dtype)


def project(attended, *weights):
    rows = attended.shape[0]
    return pl.pallas_call(
        project_kernel,
        out_shape=jax.ShapeDtypeStruct((len(weights) * rows, LANES), jnp.bfloat16),
        compiler_params=pltpu.CompilerParams(vmem_limit_bytes=SMALL),
        name="project",
    )(attended, *weights)


def total_kernel(s_ref, o_ref):
    near, heads, rows = 4, 8, 16
    half = rows // 2
    for n in range(near):
        parts = [
            s_ref[(n * heads + h) * rows : (n * heads + h + 1) * rows, :].astype(jnp.float32)
            for h in range(heads)
        ]
        total = functools.reduce(jnp.add, parts)
        for z in range(2):
            at = (z * near + n) * half
            o_ref[at : at + half, :] = total[z * half : (z + 1) * half]


def total_of(sums):
    return pl.pallas_call(
        total_kernel,
        out_shape=jax.ShapeDtypeStruct((64, LANES), jnp.float32),
        compiler_params=pltpu.CompilerParams(vmem_limit_bytes=SMALL),
        name="total",
    )(sums)


def exchange(x, axis):
    return lax.all_to_all(x, axis, 0, 0, tiled=True)


def shards(queries, keys, values, cutoffs, out_weight):
    far = SIZES[0] * SIZES[1]
    k_other = lax.ppermute(keys, "c", SWAP)
    v_other = lax.ppermute(values, "c", SWAP)
    packed = exchange(pack(queries, cutoffs, 2 * far), ("zl",) + FAR)
    pairs = (keys, values, k_other, v_other)
    away = lax.ppermute(attend(packed, 1, *pairs), "zl", SWAP)
    parts = exchange(merge(attend(packed, 0, *pairs), away), FAR)
    w_core = lax.ppermute(out_weight, "c", SWAP)
    w_chip = lax.ppermute(out_weight, "zl", SWAP)
    w_both = lax.ppermute(w_chip, "c", SWAP)
    attended = exchange(combine(parts, far), FAR)
    sums = project(attended, out_weight, w_core, w_chip, w_both)
    return total_of(exchange(sums, NEAR + HEAD))


def solution(mesh):
    fine = Mesh(mesh.devices.reshape(SIZES), AXES)
    return jax.shard_map(
        shards,
        mesh=fine,
        in_specs=(P(BLK, HEAD), P(BLK, HEAD), P(BLK, HEAD), P(BLK), P(HEAD, BLK)),
        out_specs=P(HEAD, BLK),
        check_vma=False,
    )
```

```python
import functools
import math

import jax
import jax.numpy as jnp
from jax import lax
from jax.experimental import pallas as pl
from jax.experimental.pallas import tpu as pltpu
from jax.sharding import Mesh
from jax.sharding import PartitionSpec as P

HEAD_DIM = 128
GROUP = 8
LANES = 128
WIDTH = GROUP * HEAD_DIM
PACKED = WIDTH + LANES
NEG = -1e30
FLOOR = -1e20
SCALE = math.log2(math.e) / math.sqrt(HEAD_DIM)
ROW_BLOCK = 64
REACH = 470.0
VMEM = 24 * 2**20
SMALL = 8 * 2**20

AXES = ("y", "zh", "zl", "c", "w", "x")
SIZES = (8, 2, 2, 2, 2, 4)
BLK = ("y", "zh", "zl", "c")
HEAD = ("w", "x")
FAR = ("y", "zh")
NEAR = ("zl", "c")
SWAP = ((0, 1), (1, 0))


def split(x):
    high = x.astype(jnp.bfloat16).astype(jnp.float32)
    middle = (x - high).astype(jnp.bfloat16).astype(jnp.float32)
    return high, middle, x - high - middle


def attend_kernel(chunk, whose, q_ref, k_mine, v_mine, k_other, v_other, o_ref):
    pairs = ((k_mine, v_mine), (k_other, v_other))
    rows = o_ref.shape[0]
    many = GROUP * ROW_BLOCK
    length = k_mine.shape[0]
    chip = lax.axis_index("zl")
    core = lax.axis_index("c")
    me = lax.axis_index("y") * 8 + lax.axis_index("zh") * 4 + chip * 2
    starts = ((me + core) * length, (me + 1 - core) * length)
    base = (1 - chip if whose else chip) * rows

    def load(i):
        packed = q_ref[pl.ds(pl.multiple_of(base + i * ROW_BLOCK, ROW_BLOCK), ROW_BLOCK), :]
        queries = jnp.concatenate(
            [packed[:, h * HEAD_DIM : (h + 1) * HEAD_DIM] for h in range(GROUP)], axis=0
        )
        digits = packed[:, WIDTH:].astype(jnp.float32)
        cut = digits[:, 0:1] + 64.0 * digits[:, 1:2] + 4096.0 * digits[:, 2:3]
        cut = jnp.concatenate([cut.astype(jnp.int32)] * GROUP, axis=0)
        return queries, cut

    def scores_of(queries, cut, n, at, size):
        scores = lax.dot_general(
            queries,
            pairs[n][0][at : at + size, :],
            (((1,), (1,)), ((), ())),
            preferred_element_type=jnp.float32,
        )
        places = lax.broadcasted_iota(jnp.int32, (many, size), 1)
        return jnp.where(places < cut - (starts[n] + at), scores, NEG)

    def weighed(acc, weights, n, at, size):
        wide = [pairs[n][1][at : at + size, :], jnp.ones((size, LANES), jnp.bfloat16)]
        wide = jnp.concatenate(wide, axis=1)
        weights = weights.astype(jnp.bfloat16)
        return acc + jnp.dot(weights, wide, preferred_element_type=jnp.float32)

    def store(i, acc, level=0.0):
        here = pl.ds(pl.multiple_of(i * ROW_BLOCK, ROW_BLOCK), ROW_BLOCK)
        total = acc[:, HEAD_DIM:]
        some = jnp.maximum(total, 1e-30)
        mixed = (acc[:, :HEAD_DIM] / some).astype(jnp.bfloat16)
        level = jnp.where(total > 0.0, jnp.log2(some) + level * SCALE, NEG)
        high, middle, low = split(level)
        lane = lax.broadcasted_iota(jnp.int32, (ROW_BLOCK, LANES), 1)
        stats = jnp.zeros((ROW_BLOCK, LANES), jnp.float32)
        for h in range(GROUP):
            mine = slice(h * ROW_BLOCK, (h + 1) * ROW_BLOCK)
            o_ref[here, h * HEAD_DIM : (h + 1) * HEAD_DIM] = mixed[mine]
            part = jnp.where(lane < 8, high[mine], jnp.where(lane < 16, middle[mine], low[mine]))
            stats = jnp.where((lane & 7) == h, part, stats)
        o_ref[here, WIDTH:] = jnp.where(lane < 24, stats, 0.0).astype(jnp.bfloat16)

    def quick(i, unsafe):
        queries, cut = load(i)
        acc = jnp.zeros((many, HEAD_DIM + LANES), jnp.float32)
        most = jnp.full((many, LANES), NEG, jnp.float32)
        for n in range(len(pairs)):
            for at in range(0, length, chunk):
                scores = scores_of(queries, cut, n, at, chunk)
                for t in range(0, chunk, LANES):
                    most = jnp.maximum(most, scores[:, t : t + LANES])
                acc = weighed(acc, jnp.exp2(scores * SCALE), n, at, chunk)
        store(i, acc)
        most = jnp.max(most, axis=1, keepdims=True)
        far = jnp.where(most > FLOOR, jnp.abs(most), 0.0)
        return jnp.maximum(unsafe, far)

    unsafe = jnp.zeros((many, 1), jnp.float32)
    unsafe = lax.fori_loop(0, rows // ROW_BLOCK, quick, unsafe)

    @pl.when(jnp.logical_not(jnp.max(unsafe) < REACH))
    def _():
        def exact(i, unused):
            queries, cut = load(i)
            acc = jnp.zeros((many, HEAD_DIM + LANES), jnp.float32)
            level = jnp.full((many, 1), FLOOR, jnp.float32)
            for n in range(len(pairs)):
                scores = scores_of(queries, cut, n, 0, length)
                higher = jnp.maximum(level, jnp.max(scores, axis=1, keepdims=True))
                acc = acc * jnp.exp2((level - higher) * SCALE)
                acc = weighed(acc, jnp.exp2(scores * SCALE - higher * SCALE), n, 0, length)
                level = higher
            store(i, acc, level)
            return unused

        lax.fori_loop(0, rows // ROW_BLOCK, exact, 0)


def attend(packed, whose, *pairs):
    rows = packed.shape[0] // 2
    vmem = pl.BlockSpec(memory_space=pltpu.VMEM)
    work = 4 * rows * GROUP * pairs[0].shape[0] * HEAD_DIM
    return pl.pallas_call(
        functools.partial(attend_kernel, 256, whose),
        in_specs=[vmem] * (1 + len(pairs)),
        out_specs=vmem,
        out_shape=jax.ShapeDtypeStruct((rows, PACKED), jnp.bfloat16),
        compiler_params=pltpu.CompilerParams(vmem_limit_bytes=VMEM),
        cost_estimate=pl.CostEstimate(
            flops=4 * work, bytes_accessed=2**21, transcendentals=work // 256
        ),
        name="attend",
    )(packed, *pairs)


def level_of(stats):
    stats = stats.astype(jnp.float32)
    return stats + jnp.roll(stats, -8, axis=1) + jnp.roll(stats, -16, axis=1)


def merge_kernel(a_ref, b_ref, o_ref):
    rows = 64
    lane = lax.broadcasted_iota(jnp.int32, (rows, LANES), 1)
    for at in range(0, o_ref.shape[0], rows):
        here = slice(at, at + rows)
        levels = [level_of(ref[here, WIDTH:]) for ref in (a_ref, b_ref)]
        top = jnp.maximum(*levels)
        shares = [jnp.exp2(level - top) for level in levels]
        total = shares[0] + shares[1]
        shares = [share / total for share in shares]
        for h in range(GROUP):
            head = slice(h * HEAD_DIM, (h + 1) * HEAD_DIM)
            mixed = a_ref[here, head].astype(jnp.float32) * shares[0][:, h : h + 1]
            mixed = mixed + b_ref[here, head].astype(jnp.float32) * shares[1][:, h : h + 1]
            o_ref[here, head] = mixed.astype(jnp.bfloat16)
        high, middle, low = split(top + jnp.log2(total))
        stats = jnp.where(
            lane < 8,
            high,
            jnp.where(lane < 16, jnp.roll(middle, 8, axis=1), jnp.roll(low, 16, axis=1)),
        )
        o_ref[here, WIDTH:] = jnp.where(lane < 24, stats, 0.0).astype(jnp.bfloat16)


def merge(a, b):
    return pl.pallas_call(
        merge_kernel,
        out_shape=jax.ShapeDtypeStruct(a.shape, a.dtype),
        compiler_params=pltpu.CompilerParams(vmem_limit_bytes=SMALL),
        name="merge",
    )(a, b)


def repeated(o_ref, at, block):
    twice = jnp.concatenate([block, block], axis=0)
    for top in range(0, o_ref.shape[0], twice.shape[0]):
        o_ref[top : top + twice.shape[0], at : at + block.shape[1]] = twice


def pack_kernel(q_ref, cut_ref, o_ref):
    rows = q_ref.shape[0]
    lane = lax.broadcasted_iota(jnp.int32, (rows, LANES), 1)
    row = lax.broadcasted_iota(jnp.int32, (rows, LANES), 0)
    cut = jnp.zeros((rows, LANES), jnp.int32)
    for r in range(rows):
        cut = jnp.where(row == r, cut_ref[r], cut)
    digits = jnp.where(lane == 0, cut & 63, jnp.where(lane == 1, (cut >> 6) & 63, cut >> 12))
    digits = digits.astype(jnp.float32).astype(jnp.bfloat16)
    repeated(o_ref, 0, q_ref[...])
    repeated(o_ref, WIDTH, digits)


def pack(queries, cutoffs, receivers):
    rows = queries.shape[0]
    return pl.pallas_call(
        pack_kernel,
        in_specs=[
            pl.BlockSpec(memory_space=pltpu.VMEM),
            pl.BlockSpec(memory_space=pltpu.SMEM),
        ],
        out_shape=jax.ShapeDtypeStruct((receivers * rows, PACKED), jnp.bfloat16),
        name="pack",
    )(queries, cutoffs)


def combine_kernel(p_ref, o_ref):
    rows = 8
    sources = p_ref.shape[0] // rows
    levels = []
    for n in range(sources // 2):
        level = level_of(p_ref[2 * n * rows : 2 * (n + 1) * rows, WIDTH:])
        levels += [level[:rows], level[rows:]]
    top = functools.reduce(jnp.maximum, levels)
    shares = [jnp.exp2(level - top) for level in levels]
    total = 1.0 / functools.reduce(jnp.add, shares)
    shares = [share * total for share in shares]
    sums = [jnp.zeros((rows, HEAD_DIM), jnp.float32) for _ in range(GROUP)]
    for n in range(sources // 2):
        for h in range(GROUP):
            part = p_ref[2 * n * rows : 2 * (n + 1) * rows, h * HEAD_DIM : (h + 1) * HEAD_DIM]
            part = part.astype(jnp.float32)
            sums[h] = sums[h] + part[:rows] * shares[2 * n][:, h : h + 1]
            sums[h] = sums[h] + part[rows:] * shares[2 * n + 1][:, h : h + 1]
    for h in range(GROUP):
        repeated(o_ref, h * HEAD_DIM, sums[h].astype(jnp.bfloat16))


def combine(parts, receivers):
    return pl.pallas_call(
        combine_kernel,
        out_shape=jax.ShapeDtypeStruct((8 * receivers, WIDTH), jnp.bfloat16),
        compiler_params=pltpu.CompilerParams(vmem_limit_bytes=SMALL),
        name="combine",
    )(parts)


def project_kernel(a_ref, w_ref, w_core, w_chip, w_both, o_ref):
    rows = a_ref.shape[0]
    chip = lax.axis_index("zl")
    core = lax.axis_index("c")
    attended = a_ref[...]
    for there, that, weight in (
        (chip, core, w_ref),
        (chip, 1 - core, w_core),
        (1 - chip, core, w_chip),
        (1 - chip, 1 - core, w_both),
    ):
        at = pl.multiple_of((there * 2 + that) * rows, rows)
        part = jnp.dot(attended, weight[...], preferred_element_type=jnp.float32)
        o_ref[pl.ds(at, rows), :] = part.astype(o_ref.dtype)


def project(attended, *weights):
    rows = attended.shape[0]
    return pl.pallas_call(
        project_kernel,
        out_shape=jax.ShapeDtypeStruct((len(weights) * rows, LANES), jnp.bfloat16),
        compiler_params=pltpu.CompilerParams(vmem_limit_bytes=SMALL),
        name="project",
    )(attended, *weights)


def total_kernel(s_ref, o_ref):
    near, heads, rows = 4, 8, 16
    half = rows // 2
    for n in range(near):
        parts = [
            s_ref[(n * heads + h) * rows : (n * heads + h + 1) * rows, :].astype(jnp.float32)
            for h in range(heads)
        ]
        total = functools.reduce(jnp.add, parts)
        for z in range(2):
            at = (z * near + n) * half
            o_ref[at : at + half, :] = total[z * half : (z + 1) * half]


def total_of(sums):
    return pl.pallas_call(
        total_kernel,
        out_shape=jax.ShapeDtypeStruct((64, LANES), jnp.float32),
        compiler_params=pltpu.CompilerParams(vmem_limit_bytes=SMALL),
        name="total",
    )(sums)


def exchange(x, axis):
    return lax.all_to_all(x, axis, 0, 0, tiled=True)


def shards(queries, keys, values, cutoffs, out_weight):
    far = SIZES[0] * SIZES[1]
    k_other = lax.ppermute(keys, "c", SWAP)
    v_other = lax.ppermute(values, "c", SWAP)
    packed = exchange(pack(queries, cutoffs, 2 * far), ("zl",) + FAR)
    pairs = (keys, values, k_other, v_other)
    away = lax.ppermute(attend(packed, 1, *pairs), "zl", SWAP)
    parts = exchange(merge(attend(packed, 0, *pairs), away), FAR)
    w_core = lax.ppermute(out_weight, "c", SWAP)
    w_chip = lax.ppermute(out_weight, "zl", SWAP)
    w_both = lax.ppermute(w_chip, "c", SWAP)
    attended = exchange(combine(parts, far), FAR)
    sums = project(attended, out_weight, w_core, w_chip, w_both)
    return total_of(exchange(sums, NEAR + HEAD))


def solution(mesh):
    fine = Mesh(mesh.devices.reshape(SIZES), AXES)
    return jax.shard_map(
        shards,
        mesh=fine,
        in_specs=(P(BLK, HEAD), P(BLK, HEAD), P(BLK, HEAD), P(BLK), P(HEAD, BLK)),
        out_specs=P(HEAD, BLK),
        check_vma=False,
    )
```

```python
import functools
import math

import jax
import jax.numpy as jnp
from jax import lax
from jax.experimental import pallas as pl
from jax.experimental.pallas import tpu as pltpu
from jax.sharding import Mesh
from jax.sharding import PartitionSpec as P

HEAD_DIM = 128
GROUP = 8
LANES = 128
WIDTH = GROUP * HEAD_DIM
PACKED = WIDTH + LANES
NEG = -1e30
FLOOR = -1e20
SCALE = math.log2(math.e) / math.sqrt(HEAD_DIM)
ROW_BLOCK = 64
REACH = 470.0
VMEM = 24 * 2**20
SMALL = 8 * 2**20

AXES = ("yc", "yb", "ya", "zh", "zl", "c", "w", "x")
SIZES = (2, 2, 2, 2, 2, 2, 2, 4)
BLK = ("yc", "yb", "ya", "zh", "zl", "c")
HEAD = ("w", "x")
QUERIES = ("zl", "yb", "yc", "ya", "zh")
FAR = ("zh", "yc", "yb", "ya")
NEAR = ("zl", "c")
SWAP = ((0, 1), (1, 0))


def split(x):
    high = x.astype(jnp.bfloat16).astype(jnp.float32)
    middle = (x - high).astype(jnp.bfloat16).astype(jnp.float32)
    return high, middle, x - high - middle


def attend_kernel(chunk, whose, q_ref, k_mine, v_mine, k_other, v_other, o_ref):
    pairs = ((k_mine, v_mine), (k_other, v_other))
    rows = o_ref.shape[0]
    many = GROUP * ROW_BLOCK
    length = k_mine.shape[0]
    chip = lax.axis_index("zl")
    core = lax.axis_index("c")
    me = 0
    for axis in ("yc", "yb", "ya", "zh"):
        me = me * 2 + lax.axis_index(axis)
    me = me * 4 + chip * 2
    starts = ((me + core) * length, (me + 1 - core) * length)
    base = (1 - chip if whose else chip) * rows

    def load(i):
        packed = q_ref[pl.ds(pl.multiple_of(base + i * ROW_BLOCK, ROW_BLOCK), ROW_BLOCK), :]
        queries = jnp.concatenate(
            [packed[:, h * HEAD_DIM : (h + 1) * HEAD_DIM] for h in range(GROUP)], axis=0
        )
        digits = packed[:, WIDTH:].astype(jnp.float32)
        cut = digits[:, 0:1] + 64.0 * digits[:, 1:2] + 4096.0 * digits[:, 2:3]
        cut = jnp.concatenate([cut.astype(jnp.int32)] * GROUP, axis=0)
        return queries, cut

    def scores_of(queries, cut, n, at, size):
        scores = lax.dot_general(
            queries,
            pairs[n][0][at : at + size, :],
            (((1,), (1,)), ((), ())),
            preferred_element_type=jnp.float32,
        )
        places = lax.broadcasted_iota(jnp.int32, (many, size), 1)
        return jnp.where(places < cut - (starts[n] + at), scores, NEG)

    def weighed(acc, weights, n, at, size):
        wide = [pairs[n][1][at : at + size, :], jnp.ones((size, LANES), jnp.bfloat16)]
        wide = jnp.concatenate(wide, axis=1)
        weights = weights.astype(jnp.bfloat16)
        return acc + jnp.dot(weights, wide, preferred_element_type=jnp.float32)

    def store(i, acc, level=0.0):
        here = pl.ds(pl.multiple_of(i * ROW_BLOCK, ROW_BLOCK), ROW_BLOCK)
        total = acc[:, HEAD_DIM:]
        some = jnp.maximum(total, 1e-30)
        mixed = (acc[:, :HEAD_DIM] / some).astype(jnp.bfloat16)
        level = jnp.where(total > 0.0, jnp.log2(some) + level * SCALE, NEG)
        high, middle, low = split(level)
        lane = lax.broadcasted_iota(jnp.int32, (ROW_BLOCK, LANES), 1)
        stats = jnp.zeros((ROW_BLOCK, LANES), jnp.float32)
        for h in range(GROUP):
            mine = slice(h * ROW_BLOCK, (h + 1) * ROW_BLOCK)
            o_ref[here, h * HEAD_DIM : (h + 1) * HEAD_DIM] = mixed[mine]
            part = jnp.where(lane < 8, high[mine], jnp.where(lane < 16, middle[mine], low[mine]))
            stats = jnp.where((lane & 7) == h, part, stats)
        o_ref[here, WIDTH:] = jnp.where(lane < 24, stats, 0.0).astype(jnp.bfloat16)

    def quick(i, unsafe):
        queries, cut = load(i)
        acc = jnp.zeros((many, HEAD_DIM + LANES), jnp.float32)
        most = jnp.full((many, LANES), NEG, jnp.float32)
        for n in range(len(pairs)):
            for at in range(0, length, chunk):
                scores = scores_of(queries, cut, n, at, chunk)
                for t in range(0, chunk, LANES):
                    most = jnp.maximum(most, scores[:, t : t + LANES])
                acc = weighed(acc, jnp.exp2(scores * SCALE), n, at, chunk)
        store(i, acc)
        most = jnp.max(most, axis=1, keepdims=True)
        far = jnp.where(most > FLOOR, jnp.abs(most), 0.0)
        return jnp.maximum(unsafe, far)

    unsafe = jnp.zeros((many, 1), jnp.float32)
    unsafe = lax.fori_loop(0, rows // ROW_BLOCK, quick, unsafe)

    @pl.when(jnp.logical_not(jnp.max(unsafe) < REACH))
    def _():
        def exact(i, unused):
            queries, cut = load(i)
            acc = jnp.zeros((many, HEAD_DIM + LANES), jnp.float32)
            level = jnp.full((many, 1), FLOOR, jnp.float32)
            for n in range(len(pairs)):
                scores = scores_of(queries, cut, n, 0, length)
                higher = jnp.maximum(level, jnp.max(scores, axis=1, keepdims=True))
                acc = acc * jnp.exp2((level - higher) * SCALE)
                acc = weighed(acc, jnp.exp2(scores * SCALE - higher * SCALE), n, 0, length)
                level = higher
            store(i, acc, level)
            return unused

        lax.fori_loop(0, rows // ROW_BLOCK, exact, 0)


def attend(packed, whose, *pairs):
    rows = packed.shape[0] // 2
    vmem = pl.BlockSpec(memory_space=pltpu.VMEM)
    work = 4 * rows * GROUP * pairs[0].shape[0] * HEAD_DIM
    return pl.pallas_call(
        functools.partial(attend_kernel, 256, whose),
        in_specs=[vmem] * (1 + len(pairs)),
        out_specs=vmem,
        out_shape=jax.ShapeDtypeStruct((rows, PACKED), jnp.bfloat16),
        compiler_params=pltpu.CompilerParams(vmem_limit_bytes=VMEM),
        cost_estimate=pl.CostEstimate(
            flops=4 * work, bytes_accessed=2**21, transcendentals=work // 256
        ),
        name="attend",
    )(packed, *pairs)


def level_of(stats):
    stats = stats.astype(jnp.float32)
    return stats + jnp.roll(stats, -8, axis=1) + jnp.roll(stats, -16, axis=1)


def merge_kernel(a_ref, b_ref, o_ref):
    rows = 32
    lane = lax.broadcasted_iota(jnp.int32, (rows, LANES), 1)
    for n in range(o_ref.shape[0] // rows):
        here = slice(n * rows, (n + 1) * rows)
        yb, yc = n // 2, n % 2

        def put(columns, block):
            for zh in range(2):
                at = ((zh * 2 + yc) * 2 + yb) * 16
                pair = [block[8 * zh : 8 * zh + 8], block[16 + 8 * zh : 24 + 8 * zh]]
                o_ref[at : at + 16, columns] = jnp.concatenate(pair, axis=0).astype(o_ref.dtype)

        levels = [level_of(ref[here, WIDTH:]) for ref in (a_ref, b_ref)]
        top = jnp.maximum(*levels)
        shares = [jnp.exp2(level - top) for level in levels]
        total = shares[0] + shares[1]
        shares = [share / total for share in shares]
        for h in range(GROUP):
            head = slice(h * HEAD_DIM, (h + 1) * HEAD_DIM)
            mixed = a_ref[here, head].astype(jnp.float32) * shares[0][:, h : h + 1]
            mixed = mixed + b_ref[here, head].astype(jnp.float32) * shares[1][:, h : h + 1]
            put(head, mixed)
        high, middle, low = split(top + jnp.log2(total))
        stats = jnp.where(
            lane < 8,
            high,
            jnp.where(lane < 16, jnp.roll(middle, 8, axis=1), jnp.roll(low, 16, axis=1)),
        )
        put(slice(WIDTH, PACKED), jnp.where(lane < 24, stats, 0.0))


def merge(a, b):
    return pl.pallas_call(
        merge_kernel,
        out_shape=jax.ShapeDtypeStruct(a.shape, a.dtype),
        compiler_params=pltpu.CompilerParams(vmem_limit_bytes=SMALL),
        name="merge",
    )(a, b)


def repeated(o_ref, at, block):
    twice = jnp.concatenate([block, block], axis=0)
    for top in range(0, o_ref.shape[0], twice.shape[0]):
        o_ref[top : top + twice.shape[0], at : at + block.shape[1]] = twice


def pack_kernel(q_ref, cut_ref, o_ref):
    rows = q_ref.shape[0]
    lane = lax.broadcasted_iota(jnp.int32, (rows, LANES), 1)
    row = lax.broadcasted_iota(jnp.int32, (rows, LANES), 0)
    cut = jnp.zeros((rows, LANES), jnp.int32)
    for r in range(rows):
        cut = jnp.where(row == r, cut_ref[r], cut)
    digits = jnp.where(lane == 0, cut & 63, jnp.where(lane == 1, (cut >> 6) & 63, cut >> 12))
    digits = digits.astype(jnp.float32).astype(jnp.bfloat16)
    repeated(o_ref, 0, q_ref[...])
    repeated(o_ref, WIDTH, digits)


def pack(queries, cutoffs, receivers):
    rows = queries.shape[0]
    return pl.pallas_call(
        pack_kernel,
        in_specs=[
            pl.BlockSpec(memory_space=pltpu.VMEM),
            pl.BlockSpec(memory_space=pltpu.SMEM),
        ],
        out_shape=jax.ShapeDtypeStruct((receivers * rows, PACKED), jnp.bfloat16),
        name="pack",
    )(queries, cutoffs)


def combine_kernel(p_ref, o_ref):
    rows = 8
    sources = p_ref.shape[0] // rows
    levels = []
    for n in range(sources // 2):
        level = level_of(p_ref[2 * n * rows : 2 * (n + 1) * rows, WIDTH:])
        levels += [level[:rows], level[rows:]]
    top = functools.reduce(jnp.maximum, levels)
    shares = [jnp.exp2(level - top) for level in levels]
    total = 1.0 / functools.reduce(jnp.add, shares)
    shares = [share * total for share in shares]
    sums = [jnp.zeros((rows, HEAD_DIM), jnp.float32) for _ in range(GROUP)]
    for n in range(sources // 2):
        for h in range(GROUP):
            part = p_ref[2 * n * rows : 2 * (n + 1) * rows, h * HEAD_DIM : (h + 1) * HEAD_DIM]
            part = part.astype(jnp.float32)
            sums[h] = sums[h] + part[:rows] * shares[2 * n][:, h : h + 1]
            sums[h] = sums[h] + part[rows:] * shares[2 * n + 1][:, h : h + 1]
    for h in range(GROUP):
        repeated(o_ref, h * HEAD_DIM, sums[h].astype(jnp.bfloat16))


def combine(parts, receivers):
    return pl.pallas_call(
        combine_kernel,
        out_shape=jax.ShapeDtypeStruct((8 * receivers, WIDTH), jnp.bfloat16),
        compiler_params=pltpu.CompilerParams(vmem_limit_bytes=SMALL),
        name="combine",
    )(parts)


def project_kernel(a_ref, w_ref, w_core, w_chip, w_both, o_ref):
    half = a_ref.shape[0] // 2
    chip = lax.axis_index("zl")
    core = lax.axis_index("c")
    attended = a_ref[...]
    for there, that, weight in (
        (chip, core, w_ref),
        (chip, 1 - core, w_core),
        (1 - chip, core, w_chip),
        (1 - chip, 1 - core, w_both),
    ):
        part = jnp.dot(attended, weight[...], preferred_element_type=jnp.float32)
        for y in range(half // 8):
            pair = [part[8 * y : 8 * y + 8], part[half + 8 * y : half + 8 * y + 8]]
            at = pl.multiple_of((y * 4 + there * 2 + that) * 16, 16)
            o_ref[pl.ds(at, 16), :] = jnp.concatenate(pair, axis=0).astype(o_ref.dtype)


def project(attended, *weights):
    rows = attended.shape[0]
    return pl.pallas_call(
        project_kernel,
        out_shape=jax.ShapeDtypeStruct((len(weights) * rows, LANES), jnp.bfloat16),
        compiler_params=pltpu.CompilerParams(vmem_limit_bytes=SMALL),
        name="project",
    )(attended, *weights)


def total_kernel(s_ref, o_ref):
    near, heads, rows = 4, 8, 16
    half = rows // 2
    for n in range(near):
        parts = [
            s_ref[(h * near + n) * rows : (h * near + n + 1) * rows, :].astype(jnp.float32)
            for h in range(heads)
        ]
        total = functools.reduce(jnp.add, parts)
        for z in range(2):
            at = (z * near + n) * half
            o_ref[at : at + half, :] = total[z * half : (z + 1) * half]


def total_of(sums):
    return pl.pallas_call(
        total_kernel,
        out_shape=jax.ShapeDtypeStruct((64, LANES), jnp.float32),
        compiler_params=pltpu.CompilerParams(vmem_limit_bytes=SMALL),
        name="total",
    )(sums)


def exchange(x, axis):
    return lax.all_to_all(x, axis, 0, 0, tiled=True)


def shards(queries, keys, values, cutoffs, out_weight):
    far = SIZES[0] * SIZES[1] * SIZES[2] * SIZES[3]
    k_other = lax.ppermute(keys, "c", SWAP)
    v_other = lax.ppermute(values, "c", SWAP)
    packed = exchange(pack(queries, cutoffs, 2 * far), QUERIES)
    pairs = (keys, values, k_other, v_other)
    away = lax.ppermute(attend(packed, 1, *pairs), "zl", SWAP)
    parts = exchange(merge(attend(packed, 0, *pairs), away), FAR)
    w_core = lax.ppermute(out_weight, "c", SWAP)
    w_chip = lax.ppermute(out_weight, "zl", SWAP)
    w_both = lax.ppermute(w_chip, "c", SWAP)
    attended = exchange(combine(parts, far), FAR)
    sums = project(attended, out_weight, w_core, w_chip, w_both)
    return total_of(exchange(sums, HEAD + NEAR))


def solution(mesh):
    fine = Mesh(mesh.devices.reshape(SIZES), AXES)
    return jax.shard_map(
        shards,
        mesh=fine,
        in_specs=(P(BLK, HEAD), P(BLK, HEAD), P(BLK, HEAD), P(BLK), P(HEAD, BLK)),
        out_specs=P(HEAD, BLK),
        check_vma=False,
    )
```

```python
import functools
import math

import jax
import jax.numpy as jnp
from jax import lax
from jax.experimental import pallas as pl
from jax.experimental.pallas import tpu as pltpu
from jax.sharding import Mesh
from jax.sharding import PartitionSpec as P

HEAD_DIM = 128
GROUP = 8
LANES = 128
WIDTH = GROUP * HEAD_DIM
PACKED = WIDTH + LANES
NEG = -1e30
FLOOR = -1e20
SCALE = math.log2(math.e) / math.sqrt(HEAD_DIM)
ROW_BLOCK = 64
REACH = 470.0
VMEM = 24 * 2**20
SMALL = 8 * 2**20

AXES = ("yc", "yb", "ya", "zh", "zl", "c", "w", "x")
SIZES = (2, 2, 2, 2, 2, 2, 2, 4)
BLK = ("yc", "yb", "ya", "zh", "zl", "c")
HEAD = ("w", "x")
FAR = ("zh", "yc", "yb", "ya")
QUERIES = ("zl",) + FAR
NEAR = ("zl", "c")
SWAP = ((0, 1), (1, 0))


def split(x):
    high = x.astype(jnp.bfloat16).astype(jnp.float32)
    middle = (x - high).astype(jnp.bfloat16).astype(jnp.float32)
    return high, middle, x - high - middle


def attend_kernel(chunk, whose, q_ref, k_mine, v_mine, k_other, v_other, o_ref):
    pairs = ((k_mine, v_mine), (k_other, v_other))
    rows = o_ref.shape[0]
    many = GROUP * ROW_BLOCK
    length = k_mine.shape[0]
    chip = lax.axis_index("zl")
    core = lax.axis_index("c")
    me = 0
    for axis in ("yc", "yb", "ya", "zh"):
        me = me * 2 + lax.axis_index(axis)
    me = me * 4 + chip * 2
    starts = ((me + core) * length, (me + 1 - core) * length)
    base = (1 - chip if whose else chip) * rows

    def load(i):
        packed = q_ref[pl.ds(pl.multiple_of(base + i * ROW_BLOCK, ROW_BLOCK), ROW_BLOCK), :]
        queries = jnp.concatenate(
            [packed[:, h * HEAD_DIM : (h + 1) * HEAD_DIM] for h in range(GROUP)], axis=0
        )
        digits = packed[:, WIDTH:].astype(jnp.float32)
        cut = digits[:, 0:1] + 64.0 * digits[:, 1:2] + 4096.0 * digits[:, 2:3]
        cut = jnp.concatenate([cut.astype(jnp.int32)] * GROUP, axis=0)
        return queries, cut

    def scores_of(queries, cut, n, at, size):
        scores = lax.dot_general(
            queries,
            pairs[n][0][at : at + size, :],
            (((1,), (1,)), ((), ())),
            preferred_element_type=jnp.float32,
        )
        places = lax.broadcasted_iota(jnp.int32, (many, size), 1)
        return jnp.where(places < cut - (starts[n] + at), scores, NEG)

    def weighed(acc, weights, n, at, size):
        wide = [pairs[n][1][at : at + size, :], jnp.ones((size, LANES), jnp.bfloat16)]
        wide = jnp.concatenate(wide, axis=1)
        weights = weights.astype(jnp.bfloat16)
        return acc + jnp.dot(weights, wide, preferred_element_type=jnp.float32)

    def store(i, acc, level=0.0):
        here = pl.ds(pl.multiple_of(i * ROW_BLOCK, ROW_BLOCK), ROW_BLOCK)
        total = acc[:, HEAD_DIM:]
        some = jnp.maximum(total, 1e-30)
        mixed = (acc[:, :HEAD_DIM] / some).astype(jnp.bfloat16)
        level = jnp.where(total > 0.0, jnp.log2(some) + level * SCALE, NEG)
        high, middle, low = split(level)
        lane = lax.broadcasted_iota(jnp.int32, (ROW_BLOCK, LANES), 1)
        stats = jnp.zeros((ROW_BLOCK, LANES), jnp.float32)
        for h in range(GROUP):
            mine = slice(h * ROW_BLOCK, (h + 1) * ROW_BLOCK)
            o_ref[here, h * HEAD_DIM : (h + 1) * HEAD_DIM] = mixed[mine]
            part = jnp.where(lane < 8, high[mine], jnp.where(lane < 16, middle[mine], low[mine]))
            stats = jnp.where((lane & 7) == h, part, stats)
        o_ref[here, WIDTH:] = jnp.where(lane < 24, stats, 0.0).astype(jnp.bfloat16)

    def quick(i, unsafe):
        queries, cut = load(i)
        acc = jnp.zeros((many, HEAD_DIM + LANES), jnp.float32)
        most = jnp.full((many, LANES), NEG, jnp.float32)
        for n in range(len(pairs)):
            for at in range(0, length, chunk):
                scores = scores_of(queries, cut, n, at, chunk)
                for t in range(0, chunk, LANES):
                    most = jnp.maximum(most, scores[:, t : t + LANES])
                acc = weighed(acc, jnp.exp2(scores * SCALE), n, at, chunk)
        store(i, acc)
        most = jnp.max(most, axis=1, keepdims=True)
        far = jnp.where(most > FLOOR, jnp.abs(most), 0.0)
        return jnp.maximum(unsafe, far)

    unsafe = jnp.zeros((many, 1), jnp.float32)
    unsafe = lax.fori_loop(0, rows // ROW_BLOCK, quick, unsafe)

    @pl.when(jnp.logical_not(jnp.max(unsafe) < REACH))
    def _():
        def exact(i, unused):
            queries, cut = load(i)
            acc = jnp.zeros((many, HEAD_DIM + LANES), jnp.float32)
            level = jnp.full((many, 1), FLOOR, jnp.float32)
            for n in range(len(pairs)):
                scores = scores_of(queries, cut, n, 0, length)
                higher = jnp.maximum(level, jnp.max(scores, axis=1, keepdims=True))
                acc = acc * jnp.exp2((level - higher) * SCALE)
                acc = weighed(acc, jnp.exp2(scores * SCALE - higher * SCALE), n, 0, length)
                level = higher
            store(i, acc, level)
            return unused

        lax.fori_loop(0, rows // ROW_BLOCK, exact, 0)


def attend(packed, whose, *pairs):
    rows = packed.shape[0] // 2
    vmem = pl.BlockSpec(memory_space=pltpu.VMEM)
    work = 4 * rows * GROUP * pairs[0].shape[0] * HEAD_DIM
    return pl.pallas_call(
        functools.partial(attend_kernel, 256, whose),
        in_specs=[vmem] * (1 + len(pairs)),
        out_specs=vmem,
        out_shape=jax.ShapeDtypeStruct((rows, PACKED), jnp.bfloat16),
        compiler_params=pltpu.CompilerParams(vmem_limit_bytes=VMEM),
        cost_estimate=pl.CostEstimate(
            flops=4 * work, bytes_accessed=2**21, transcendentals=work // 256
        ),
        name="attend",
    )(packed, *pairs)


def level_of(stats):
    stats = stats.astype(jnp.float32)
    return stats + jnp.roll(stats, -8, axis=1) + jnp.roll(stats, -16, axis=1)


def merge_kernel(a_ref, b_ref, o_ref):
    rows = 64
    lane = lax.broadcasted_iota(jnp.int32, (rows, LANES), 1)
    for at in range(0, o_ref.shape[0], rows):
        here = slice(at, at + rows)
        levels = [level_of(ref[here, WIDTH:]) for ref in (a_ref, b_ref)]
        top = jnp.maximum(*levels)
        shares = [jnp.exp2(level - top) for level in levels]
        total = shares[0] + shares[1]
        shares = [share / total for share in shares]
        for h in range(GROUP):
            head = slice(h * HEAD_DIM, (h + 1) * HEAD_DIM)
            mixed = a_ref[here, head].astype(jnp.float32) * shares[0][:, h : h + 1]
            mixed = mixed + b_ref[here, head].astype(jnp.float32) * shares[1][:, h : h + 1]
            o_ref[here, head] = mixed.astype(jnp.bfloat16)
        high, middle, low = split(top + jnp.log2(total))
        stats = jnp.where(
            lane < 8,
            high,
            jnp.where(lane < 16, jnp.roll(middle, 8, axis=1), jnp.roll(low, 16, axis=1)),
        )
        o_ref[here, WIDTH:] = jnp.where(lane < 24, stats, 0.0).astype(jnp.bfloat16)


def merge(a, b):
    return pl.pallas_call(
        merge_kernel,
        out_shape=jax.ShapeDtypeStruct(a.shape, a.dtype),
        compiler_params=pltpu.CompilerParams(vmem_limit_bytes=SMALL),
        name="merge",
    )(a, b)


def repeated(o_ref, at, block):
    twice = jnp.concatenate([block, block], axis=0)
    for top in range(0, o_ref.shape[0], twice.shape[0]):
        o_ref[top : top + twice.shape[0], at : at + block.shape[1]] = twice


def pack_kernel(q_ref, cut_ref, o_ref):
    rows = q_ref.shape[0]
    lane = lax.broadcasted_iota(jnp.int32, (rows, LANES), 1)
    row = lax.broadcasted_iota(jnp.int32, (rows, LANES), 0)
    cut = jnp.zeros((rows, LANES), jnp.int32)
    for r in range(rows):
        cut = jnp.where(row == r, cut_ref[r], cut)
    digits = jnp.where(lane == 0, cut & 63, jnp.where(lane == 1, (cut >> 6) & 63, cut >> 12))
    digits = digits.astype(jnp.float32).astype(jnp.bfloat16)
    repeated(o_ref, 0, q_ref[...])
    repeated(o_ref, WIDTH, digits)


def pack(queries, cutoffs, receivers):
    rows = queries.shape[0]
    return pl.pallas_call(
        pack_kernel,
        in_specs=[
            pl.BlockSpec(memory_space=pltpu.VMEM),
            pl.BlockSpec(memory_space=pltpu.SMEM),
        ],
        out_shape=jax.ShapeDtypeStruct((receivers * rows, PACKED), jnp.bfloat16),
        name="pack",
    )(queries, cutoffs)


def combine_kernel(p_ref, o_ref):
    rows = 8
    sources = p_ref.shape[0] // rows
    levels = []
    for n in range(sources // 2):
        level = level_of(p_ref[2 * n * rows : 2 * (n + 1) * rows, WIDTH:])
        levels += [level[:rows], level[rows:]]
    top = functools.reduce(jnp.maximum, levels)
    shares = [jnp.exp2(level - top) for level in levels]
    total = 1.0 / functools.reduce(jnp.add, shares)
    shares = [share * total for share in shares]
    sums = [jnp.zeros((rows, HEAD_DIM), jnp.float32) for _ in range(GROUP)]
    for n in range(sources // 2):
        for h in range(GROUP):
            part = p_ref[2 * n * rows : 2 * (n + 1) * rows, h * HEAD_DIM : (h + 1) * HEAD_DIM]
            part = part.astype(jnp.float32)
            sums[h] = sums[h] + part[:rows] * shares[2 * n][:, h : h + 1]
            sums[h] = sums[h] + part[rows:] * shares[2 * n + 1][:, h : h + 1]
    for h in range(GROUP):
        repeated(o_ref, h * HEAD_DIM, sums[h].astype(jnp.bfloat16))


def combine(parts, receivers):
    return pl.pallas_call(
        combine_kernel,
        out_shape=jax.ShapeDtypeStruct((8 * receivers, WIDTH), jnp.bfloat16),
        compiler_params=pltpu.CompilerParams(vmem_limit_bytes=SMALL),
        name="combine",
    )(parts)


def project_kernel(a_ref, w_ref, w_core, w_chip, w_both, o_ref):
    half = a_ref.shape[0] // 2
    chip = lax.axis_index("zl")
    core = lax.axis_index("c")
    attended = a_ref[...]
    for there, that, weight in (
        (chip, core, w_ref),
        (chip, 1 - core, w_core),
        (1 - chip, core, w_chip),
        (1 - chip, 1 - core, w_both),
    ):
        part = jnp.dot(attended, weight[...], preferred_element_type=jnp.float32)
        for y in range(half // 8):
            pair = [part[8 * y : 8 * y + 8], part[half + 8 * y : half + 8 * y + 8]]
            at = pl.multiple_of((y * 4 + there * 2 + that) * 16, 16)
            o_ref[pl.ds(at, 16), :] = jnp.concatenate(pair, axis=0).astype(o_ref.dtype)


def project(attended, *weights):
    rows = attended.shape[0]
    return pl.pallas_call(
        project_kernel,
        out_shape=jax.ShapeDtypeStruct((len(weights) * rows, LANES), jnp.bfloat16),
        compiler_params=pltpu.CompilerParams(vmem_limit_bytes=SMALL),
        name="project",
    )(attended, *weights)


def total_kernel(s_ref, o_ref):
    near, heads, rows = 4, 8, 16
    half = rows // 2
    for n in range(near):
        parts = [
            s_ref[(h * near + n) * rows : (h * near + n + 1) * rows, :].astype(jnp.float32)
            for h in range(heads)
        ]
        total = functools.reduce(jnp.add, parts)
        for z in range(2):
            at = (z * near + n) * half
            o_ref[at : at + half, :] = total[z * half : (z + 1) * half]


def total_of(sums):
    return pl.pallas_call(
        total_kernel,
        out_shape=jax.ShapeDtypeStruct((64, LANES), jnp.float32),
        compiler_params=pltpu.CompilerParams(vmem_limit_bytes=SMALL),
        name="total",
    )(sums)


def exchange(x, axis):
    return lax.all_to_all(x, axis, 0, 0, tiled=True)


def shards(queries, keys, values, cutoffs, out_weight):
    far = SIZES[0] * SIZES[1] * SIZES[2] * SIZES[3]
    k_other = lax.ppermute(keys, "c", SWAP)
    v_other = lax.ppermute(values, "c", SWAP)
    packed = exchange(pack(queries, cutoffs, 2 * far), QUERIES)
    pairs = (keys, values, k_other, v_other)
    away = lax.ppermute(attend(packed, 1, *pairs), "zl", SWAP)
    parts = exchange(merge(attend(packed, 0, *pairs), away), FAR)
    w_core = lax.ppermute(out_weight, "c", SWAP)
    w_chip = lax.ppermute(out_weight, "zl", SWAP)
    w_both = lax.ppermute(w_chip, "c", SWAP)
    attended = exchange(combine(parts, far), FAR)
    sums = project(attended, out_weight, w_core, w_chip, w_both)
    return total_of(exchange(sums, HEAD + NEAR))


def solution(mesh):
    fine = Mesh(mesh.devices.reshape(SIZES), AXES)
    return jax.shard_map(
        shards,
        mesh=fine,
        in_specs=(P(BLK, HEAD), P(BLK, HEAD), P(BLK, HEAD), P(BLK), P(HEAD, BLK)),
        out_specs=P(HEAD, BLK),
        check_vma=False,
    )
```

```python
import functools
import math

import jax
import jax.numpy as jnp
from jax import lax
from jax.experimental import pallas as pl
from jax.experimental.pallas import tpu as pltpu
from jax.sharding import Mesh
from jax.sharding import PartitionSpec as P

HEAD_DIM = 128
GROUP = 8
LANES = 128
WIDTH = GROUP * HEAD_DIM
PACKED = WIDTH + LANES
NEG = -1e30
FLOOR = -1e20
SCALE = math.log2(math.e) / math.sqrt(HEAD_DIM)
ROW_BLOCK = 64
REACH = 470.0
VMEM = 24 * 2**20
SMALL = 8 * 2**20

AXES = ("yc", "yb", "ya", "zh", "zl", "c", "w", "x")
SIZES = (2, 2, 2, 2, 2, 2, 2, 4)
BLK = ("yc", "yb", "ya", "zh", "zl", "c")
HEAD = ("w", "x")
QUERIES = ("zl", "yb", "yc", "ya", "zh")
FAR = ("zh", "yc", "yb", "ya")
NEAR = ("zl", "c")
SWAP = ((0, 1), (1, 0))


def split(x):
    high = x.astype(jnp.bfloat16).astype(jnp.float32)
    middle = (x - high).astype(jnp.bfloat16).astype(jnp.float32)
    return high, middle, x - high - middle


def attend_kernel(chunk, whose, q_ref, k_mine, v_mine, k_other, v_other, o_ref):
    pairs = ((k_mine, v_mine), (k_other, v_other))
    rows = o_ref.shape[0]
    many = GROUP * ROW_BLOCK
    length = k_mine.shape[0]
    chip = lax.axis_index("zl")
    core = lax.axis_index("c")
    me = 0
    for axis in ("yc", "yb", "ya", "zh"):
        me = me * 2 + lax.axis_index(axis)
    me = me * 4 + chip * 2
    starts = ((me + core) * length, (me + 1 - core) * length)
    base = (1 - chip if whose else chip) * rows

    def load(i):
        packed = q_ref[pl.ds(pl.multiple_of(base + i * ROW_BLOCK, ROW_BLOCK), ROW_BLOCK), :]
        queries = jnp.concatenate(
            [packed[:, h * HEAD_DIM : (h + 1) * HEAD_DIM] for h in range(GROUP)], axis=0
        )
        digits = packed[:, WIDTH:].astype(jnp.float32)
        cut = digits[:, 0:1] + 64.0 * digits[:, 1:2] + 4096.0 * digits[:, 2:3]
        cut = jnp.concatenate([cut.astype(jnp.int32)] * GROUP, axis=0)
        return queries, cut

    def scores_of(queries, cut, n, at, size):
        scores = lax.dot_general(
            queries,
            pairs[n][0][at : at + size, :],
            (((1,), (1,)), ((), ())),
            preferred_element_type=jnp.float32,
        )
        places = lax.broadcasted_iota(jnp.int32, (many, size), 1)
        return jnp.where(places < cut - (starts[n] + at), scores, NEG)

    def weighed(acc, weights, n, at, size):
        wide = [pairs[n][1][at : at + size, :], jnp.ones((size, LANES), jnp.bfloat16)]
        wide = jnp.concatenate(wide, axis=1)
        weights = weights.astype(jnp.bfloat16)
        return acc + jnp.dot(weights, wide, preferred_element_type=jnp.float32)

    def store(i, acc, level=0.0):
        here = pl.ds(pl.multiple_of(i * ROW_BLOCK, ROW_BLOCK), ROW_BLOCK)
        total = acc[:, HEAD_DIM:]
        some = jnp.maximum(total, 1e-30)
        mixed = (acc[:, :HEAD_DIM] / some).astype(jnp.bfloat16)
        level = jnp.where(total > 0.0, jnp.log2(some) + level * SCALE, NEG)
        high, middle, low = split(level)
        lane = lax.broadcasted_iota(jnp.int32, (ROW_BLOCK, LANES), 1)
        stats = jnp.zeros((ROW_BLOCK, LANES), jnp.float32)
        for h in range(GROUP):
            mine = slice(h * ROW_BLOCK, (h + 1) * ROW_BLOCK)
            o_ref[here, h * HEAD_DIM : (h + 1) * HEAD_DIM] = mixed[mine]
            part = jnp.where(lane < 8, high[mine], jnp.where(lane < 16, middle[mine], low[mine]))
            stats = jnp.where((lane & 7) == h, part, stats)
        o_ref[here, WIDTH:] = jnp.where(lane < 24, stats, 0.0).astype(jnp.bfloat16)

    def quick(i, unsafe):
        queries, cut = load(i)
        acc = jnp.zeros((many, HEAD_DIM + LANES), jnp.float32)
        most = jnp.full((many, LANES), NEG, jnp.float32)
        for n in range(len(pairs)):
            for at in range(0, length, chunk):
                scores = scores_of(queries, cut, n, at, chunk)
                for t in range(0, chunk, LANES):
                    most = jnp.maximum(most, scores[:, t : t + LANES])
                acc = weighed(acc, jnp.exp2(scores * SCALE), n, at, chunk)
        store(i, acc)
        most = jnp.max(most, axis=1, keepdims=True)
        far = jnp.where(most > FLOOR, jnp.abs(most), 0.0)
        return jnp.maximum(unsafe, far)

    unsafe = jnp.zeros((many, 1), jnp.float32)
    unsafe = lax.fori_loop(0, rows // ROW_BLOCK, quick, unsafe, unroll=True)

    @pl.when(jnp.logical_not(jnp.max(unsafe) < REACH))
    def _():
        def exact(i, unused):
            queries, cut = load(i)
            acc = jnp.zeros((many, HEAD_DIM + LANES), jnp.float32)
            level = jnp.full((many, 1), FLOOR, jnp.float32)
            for n in range(len(pairs)):
                scores = scores_of(queries, cut, n, 0, length)
                higher = jnp.maximum(level, jnp.max(scores, axis=1, keepdims=True))
                acc = acc * jnp.exp2((level - higher) * SCALE)
                acc = weighed(acc, jnp.exp2(scores * SCALE - higher * SCALE), n, 0, length)
                level = higher
            store(i, acc, level)
            return unused

        lax.fori_loop(0, rows // ROW_BLOCK, exact, 0)


def attend(packed, whose, *pairs):
    rows = packed.shape[0] // 2
    vmem = pl.BlockSpec(memory_space=pltpu.VMEM)
    work = 4 * rows * GROUP * pairs[0].shape[0] * HEAD_DIM
    return pl.pallas_call(
        functools.partial(attend_kernel, 256, whose),
        in_specs=[vmem] * (1 + len(pairs)),
        out_specs=vmem,
        out_shape=jax.ShapeDtypeStruct((rows, PACKED), jnp.bfloat16),
        compiler_params=pltpu.CompilerParams(vmem_limit_bytes=VMEM),
        cost_estimate=pl.CostEstimate(
            flops=4 * work, bytes_accessed=2**21, transcendentals=work // 256
        ),
        name="attend",
    )(packed, *pairs)


def level_of(stats):
    stats = stats.astype(jnp.float32)
    return stats + jnp.roll(stats, -8, axis=1) + jnp.roll(stats, -16, axis=1)


def merge_kernel(a_ref, b_ref, o_ref):
    rows = 32
    lane = lax.broadcasted_iota(jnp.int32, (rows, LANES), 1)
    for n in range(o_ref.shape[0] // rows):
        here = slice(n * rows, (n + 1) * rows)
        yb, yc = n // 2, n % 2

        def put(columns, block):
            for zh in range(2):
                at = ((zh * 2 + yc) * 2 + yb) * 16
                pair = [block[8 * zh : 8 * zh + 8], block[16 + 8 * zh : 24 + 8 * zh]]
                o_ref[at : at + 16, columns] = jnp.concatenate(pair, axis=0).astype(o_ref.dtype)

        levels = [level_of(ref[here, WIDTH:]) for ref in (a_ref, b_ref)]
        top = jnp.maximum(*levels)
        shares = [jnp.exp2(level - top) for level in levels]
        total = shares[0] + shares[1]
        shares = [share / total for share in shares]
        for h in range(GROUP):
            head = slice(h * HEAD_DIM, (h + 1) * HEAD_DIM)
            mixed = a_ref[here, head].astype(jnp.float32) * shares[0][:, h : h + 1]
            mixed = mixed + b_ref[here, head].astype(jnp.float32) * shares[1][:, h : h + 1]
            put(head, mixed)
        high, middle, low = split(top + jnp.log2(total))
        stats = jnp.where(
            lane < 8,
            high,
            jnp.where(lane < 16, jnp.roll(middle, 8, axis=1), jnp.roll(low, 16, axis=1)),
        )
        put(slice(WIDTH, PACKED), jnp.where(lane < 24, stats, 0.0))


def merge(a, b):
    return pl.pallas_call(
        merge_kernel,
        out_shape=jax.ShapeDtypeStruct(a.shape, a.dtype),
        compiler_params=pltpu.CompilerParams(vmem_limit_bytes=SMALL),
        name="merge",
    )(a, b)


def repeated(o_ref, at, block):
    twice = jnp.concatenate([block, block], axis=0)
    for top in range(0, o_ref.shape[0], twice.shape[0]):
        o_ref[top : top + twice.shape[0], at : at + block.shape[1]] = twice


def pack_kernel(q_ref, cut_ref, o_ref):
    rows = q_ref.shape[0]
    lane = lax.broadcasted_iota(jnp.int32, (rows, LANES), 1)
    row = lax.broadcasted_iota(jnp.int32, (rows, LANES), 0)
    cut = jnp.zeros((rows, LANES), jnp.int32)
    for r in range(rows):
        cut = jnp.where(row == r, cut_ref[r], cut)
    digits = jnp.where(lane == 0, cut & 63, jnp.where(lane == 1, (cut >> 6) & 63, cut >> 12))
    digits = digits.astype(jnp.float32).astype(jnp.bfloat16)
    repeated(o_ref, 0, q_ref[...])
    repeated(o_ref, WIDTH, digits)


def pack(queries, cutoffs, receivers):
    rows = queries.shape[0]
    return pl.pallas_call(
        pack_kernel,
        in_specs=[
            pl.BlockSpec(memory_space=pltpu.VMEM),
            pl.BlockSpec(memory_space=pltpu.SMEM),
        ],
        out_shape=jax.ShapeDtypeStruct((receivers * rows, PACKED), jnp.bfloat16),
        name="pack",
    )(queries, cutoffs)


def combine_kernel(p_ref, o_ref):
    rows = 8
    sources = p_ref.shape[0] // rows
    levels = []
    for n in range(sources // 2):
        level = level_of(p_ref[2 * n * rows : 2 * (n + 1) * rows, WIDTH:])
        levels += [level[:rows], level[rows:]]
    top = functools.reduce(jnp.maximum, levels)
    shares = [jnp.exp2(level - top) for level in levels]
    total = 1.0 / functools.reduce(jnp.add, shares)
    shares = [share * total for share in shares]
    sums = [jnp.zeros((rows, HEAD_DIM), jnp.float32) for _ in range(GROUP)]
    for n in range(sources // 2):
        for h in range(GROUP):
            part = p_ref[2 * n * rows : 2 * (n + 1) * rows, h * HEAD_DIM : (h + 1) * HEAD_DIM]
            part = part.astype(jnp.float32)
            sums[h] = sums[h] + part[:rows] * shares[2 * n][:, h : h + 1]
            sums[h] = sums[h] + part[rows:] * shares[2 * n + 1][:, h : h + 1]
    for h in range(GROUP):
        repeated(o_ref, h * HEAD_DIM, sums[h].astype(jnp.bfloat16))


def combine(parts, receivers):
    return pl.pallas_call(
        combine_kernel,
        out_shape=jax.ShapeDtypeStruct((8 * receivers, WIDTH), jnp.bfloat16),
        compiler_params=pltpu.CompilerParams(vmem_limit_bytes=SMALL),
        name="combine",
    )(parts)


def project_kernel(a_ref, w_ref, w_core, w_chip, w_both, o_ref):
    half = a_ref.shape[0] // 2
    chip = lax.axis_index("zl")
    core = lax.axis_index("c")
    attended = a_ref[...]
    for there, that, weight in (
        (chip, core, w_ref),
        (chip, 1 - core, w_core),
        (1 - chip, core, w_chip),
        (1 - chip, 1 - core, w_both),
    ):
        part = jnp.dot(attended, weight[...], preferred_element_type=jnp.float32)
        for y in range(half // 8):
            pair = [part[8 * y : 8 * y + 8], part[half + 8 * y : half + 8 * y + 8]]
            at = pl.multiple_of((y * 4 + there * 2 + that) * 16, 16)
            o_ref[pl.ds(at, 16), :] = jnp.concatenate(pair, axis=0).astype(o_ref.dtype)


def project(attended, *weights):
    rows = attended.shape[0]
    return pl.pallas_call(
        project_kernel,
        out_shape=jax.ShapeDtypeStruct((len(weights) * rows, LANES), jnp.bfloat16),
        compiler_params=pltpu.CompilerParams(vmem_limit_bytes=SMALL),
        name="project",
    )(attended, *weights)


def total_kernel(s_ref, o_ref):
    near, heads, rows = 4, 8, 16
    half = rows // 2
    for n in range(near):
        parts = [
            s_ref[(h * near + n) * rows : (h * near + n + 1) * rows, :].astype(jnp.float32)
            for h in range(heads)
        ]
        total = functools.reduce(jnp.add, parts)
        for z in range(2):
            at = (z * near + n) * half
            o_ref[at : at + half, :] = total[z * half : (z + 1) * half]


def total_of(sums):
    return pl.pallas_call(
        total_kernel,
        out_shape=jax.ShapeDtypeStruct((64, LANES), jnp.float32),
        compiler_params=pltpu.CompilerParams(vmem_limit_bytes=SMALL),
        name="total",
    )(sums)


def exchange(x, axis):
    return lax.all_to_all(x, axis, 0, 0, tiled=True)


def shards(queries, keys, values, cutoffs, out_weight):
    far = SIZES[0] * SIZES[1] * SIZES[2] * SIZES[3]
    k_other = lax.ppermute(keys, "c", SWAP)
    v_other = lax.ppermute(values, "c", SWAP)
    packed = exchange(pack(queries, cutoffs, 2 * far), QUERIES)
    pairs = (keys, values, k_other, v_other)
    away = lax.ppermute(attend(packed, 1, *pairs), "zl", SWAP)
    parts = exchange(merge(attend(packed, 0, *pairs), away), FAR)
    w_core = lax.ppermute(out_weight, "c", SWAP)
    w_chip = lax.ppermute(out_weight, "zl", SWAP)
    w_both = lax.ppermute(w_chip, "c", SWAP)
    attended = exchange(combine(parts, far), FAR)
    sums = project(attended, out_weight, w_core, w_chip, w_both)
    return total_of(exchange(sums, HEAD + NEAR))


def solution(mesh):
    fine = Mesh(mesh.devices.reshape(SIZES), AXES)
    return jax.shard_map(
        shards,
        mesh=fine,
        in_specs=(P(BLK, HEAD), P(BLK, HEAD), P(BLK, HEAD), P(BLK), P(HEAD, BLK)),
        out_specs=P(HEAD, BLK),
        check_vma=False,
    )
```

```python
import functools
import math

import jax
import jax.numpy as jnp
from jax import lax
from jax.experimental import pallas as pl
from jax.experimental.pallas import tpu as pltpu
from jax.sharding import Mesh
from jax.sharding import PartitionSpec as P

HEAD_DIM = 128
GROUP = 8
LANES = 128
WIDTH = GROUP * HEAD_DIM
PACKED = WIDTH + LANES
NEG = -1e30
FLOOR = -1e20
SCALE = math.log2(math.e) / math.sqrt(HEAD_DIM)
ROW_BLOCK = 64
REACH = 470.0
VMEM = 24 * 2**20
SMALL = 8 * 2**20

AXES = ("yc", "yb", "ya", "zh", "zl", "c", "w", "x")
SIZES = (2, 2, 2, 2, 2, 2, 2, 4)
BLK = ("yc", "yb", "ya", "zh", "zl", "c")
HEAD = ("w", "x")
QUERIES = ("zl", "yb", "yc", "ya", "zh")
FAR = ("zh", "yc", "yb", "ya")
NEAR = ("zl", "c")
SWAP = ((0, 1), (1, 0))


def split(x):
    high = x.astype(jnp.bfloat16).astype(jnp.float32)
    middle = (x - high).astype(jnp.bfloat16).astype(jnp.float32)
    return high, middle, x - high - middle


def attend_kernel(chunk, whose, q_ref, k_mine, v_mine, k_other, v_other, o_ref):
    pairs = ((k_mine, v_mine), (k_other, v_other))
    rows = o_ref.shape[0]
    many = GROUP * ROW_BLOCK
    length = k_mine.shape[0]
    chip = lax.axis_index("zl")
    core = lax.axis_index("c")
    me = 0
    for axis in ("yc", "yb", "ya", "zh"):
        me = me * 2 + lax.axis_index(axis)
    me = me * 4 + chip * 2
    starts = ((me + core) * length, (me + 1 - core) * length)
    base = (1 - chip if whose else chip) * rows

    def load(i):
        packed = q_ref[pl.ds(pl.multiple_of(base + i * ROW_BLOCK, ROW_BLOCK), ROW_BLOCK), :]
        queries = jnp.concatenate(
            [packed[:, h * HEAD_DIM : (h + 1) * HEAD_DIM] for h in range(GROUP)], axis=0
        )
        digits = packed[:, WIDTH:].astype(jnp.float32)
        cut = digits[:, 0:1] + 64.0 * digits[:, 1:2] + 4096.0 * digits[:, 2:3]
        cut = jnp.concatenate([cut.astype(jnp.int32)] * GROUP, axis=0)
        return queries, cut

    def scores_of(queries, cut, n, at, size):
        scores = lax.dot_general(
            queries,
            pairs[n][0][at : at + size, :],
            (((1,), (1,)), ((), ())),
            preferred_element_type=jnp.float32,
        )
        places = lax.broadcasted_iota(jnp.int32, (many, size), 1)
        return jnp.where(places < cut - (starts[n] + at), scores, NEG)

    def weighed(acc, weights, n, at, size):
        wide = [pairs[n][1][at : at + size, :], jnp.ones((size, LANES), jnp.bfloat16)]
        wide = jnp.concatenate(wide, axis=1)
        weights = weights.astype(jnp.bfloat16)
        return acc + jnp.dot(weights, wide, preferred_element_type=jnp.float32)

    def store(i, acc, level=0.0):
        here = pl.ds(pl.multiple_of(i * ROW_BLOCK, ROW_BLOCK), ROW_BLOCK)
        total = acc[:, HEAD_DIM:]
        some = jnp.maximum(total, 1e-30)
        mixed = (acc[:, :HEAD_DIM] / some).astype(jnp.bfloat16)
        level = jnp.where(total > 0.0, jnp.log2(some) + level * SCALE, NEG)
        high, middle, low = split(level)
        lane = lax.broadcasted_iota(jnp.int32, (ROW_BLOCK, LANES), 1)
        stats = jnp.zeros((ROW_BLOCK, LANES), jnp.float32)
        for h in range(GROUP):
            mine = slice(h * ROW_BLOCK, (h + 1) * ROW_BLOCK)
            o_ref[here, h * HEAD_DIM : (h + 1) * HEAD_DIM] = mixed[mine]
            part = jnp.where(lane < 8, high[mine], jnp.where(lane < 16, middle[mine], low[mine]))
            stats = jnp.where((lane & 7) == h, part, stats)
        o_ref[here, WIDTH:] = jnp.where(lane < 24, stats, 0.0).astype(jnp.bfloat16)

    def quick(i, unsafe):
        queries, cut = load(i)
        acc = jnp.zeros((many, HEAD_DIM + LANES), jnp.float32)
        most = jnp.full((many, LANES), NEG, jnp.float32)
        for n in range(len(pairs)):
            for at in range(0, length, chunk):
                scores = scores_of(queries, cut, n, at, chunk)
                for t in range(0, chunk, LANES):
                    most = jnp.maximum(most, scores[:, t : t + LANES])
                acc = weighed(acc, jnp.exp2(scores * SCALE), n, at, chunk)
        store(i, acc)
        most = jnp.max(most, axis=1, keepdims=True)
        far = jnp.where(most > FLOOR, jnp.abs(most), 0.0)
        return jnp.maximum(unsafe, far)

    unsafe = jnp.zeros((many, 1), jnp.float32)
    unsafe = lax.fori_loop(0, rows // ROW_BLOCK, quick, unsafe, unroll=True)

    @pl.when(jnp.logical_not(jnp.max(unsafe) < REACH))
    def _():
        def exact(i, unused):
            queries, cut = load(i)
            acc = jnp.zeros((many, HEAD_DIM + LANES), jnp.float32)
            level = jnp.full((many, 1), FLOOR, jnp.float32)
            for n in range(len(pairs)):
                scores = scores_of(queries, cut, n, 0, length)
                higher = jnp.maximum(level, jnp.max(scores, axis=1, keepdims=True))
                acc = acc * jnp.exp2((level - higher) * SCALE)
                acc = weighed(acc, jnp.exp2(scores * SCALE - higher * SCALE), n, 0, length)
                level = higher
            store(i, acc, level)
            return unused

        lax.fori_loop(0, rows // ROW_BLOCK, exact, 0)


def attend(packed, whose, *pairs):
    rows = packed.shape[0] // 2
    vmem = pl.BlockSpec(memory_space=pltpu.VMEM)
    work = 4 * rows * GROUP * pairs[0].shape[0] * HEAD_DIM
    return pl.pallas_call(
        functools.partial(attend_kernel, 256, whose),
        in_specs=[vmem] * (1 + len(pairs)),
        out_specs=vmem,
        out_shape=jax.ShapeDtypeStruct((rows, PACKED), jnp.bfloat16),
        compiler_params=pltpu.CompilerParams(vmem_limit_bytes=VMEM),
        cost_estimate=pl.CostEstimate(
            flops=4 * work, bytes_accessed=2**21, transcendentals=work // 256
        ),
        name="attend",
    )(packed, *pairs)


def level_of(stats):
    stats = stats.astype(jnp.float32)
    return stats + jnp.roll(stats, -8, axis=1) + jnp.roll(stats, -16, axis=1)


def merge_kernel(a_ref, b_ref, o_ref):
    rows = 32
    lane = lax.broadcasted_iota(jnp.int32, (rows, LANES), 1)
    for n in range(o_ref.shape[0] // rows):
        here = slice(n * rows, (n + 1) * rows)
        yb, yc = n // 2, n % 2

        def put(columns, block):
            for zh in range(2):
                at = ((zh * 2 + yc) * 2 + yb) * 16
                pair = [block[8 * zh : 8 * zh + 8], block[16 + 8 * zh : 24 + 8 * zh]]
                o_ref[at : at + 16, columns] = jnp.concatenate(pair, axis=0).astype(o_ref.dtype)

        levels = [level_of(ref[here, WIDTH:]) for ref in (a_ref, b_ref)]
        top = jnp.maximum(*levels)
        shares = [jnp.exp2(level - top) for level in levels]
        total = shares[0] + shares[1]
        shares = [share / total for share in shares]
        for h in range(GROUP):
            head = slice(h * HEAD_DIM, (h + 1) * HEAD_DIM)
            mixed = a_ref[here, head].astype(jnp.float32) * shares[0][:, h : h + 1]
            mixed = mixed + b_ref[here, head].astype(jnp.float32) * shares[1][:, h : h + 1]
            put(head, mixed)
        high, middle, low = split(top + jnp.log2(total))
        stats = jnp.where(
            lane < 8,
            high,
            jnp.where(lane < 16, jnp.roll(middle, 8, axis=1), jnp.roll(low, 16, axis=1)),
        )
        put(slice(WIDTH, PACKED), jnp.where(lane < 24, stats, 0.0))


def merge(a, b):
    return pl.pallas_call(
        merge_kernel,
        out_shape=jax.ShapeDtypeStruct(a.shape, a.dtype),
        compiler_params=pltpu.CompilerParams(vmem_limit_bytes=SMALL),
        name="merge",
    )(a, b)


def repeated(o_ref, at, block):
    twice = jnp.concatenate([block, block], axis=0)
    for top in range(0, o_ref.shape[0], twice.shape[0]):
        o_ref[top : top + twice.shape[0], at : at + block.shape[1]] = twice


def pack_kernel(q_ref, cut_ref, o_ref):
    rows = q_ref.shape[0]
    lane = lax.broadcasted_iota(jnp.int32, (rows, LANES), 1)
    row = lax.broadcasted_iota(jnp.int32, (rows, LANES), 0)
    cut = jnp.zeros((rows, LANES), jnp.int32)
    for r in range(rows):
        cut = jnp.where(row == r, cut_ref[r], cut)
    digits = jnp.where(lane == 0, cut & 63, jnp.where(lane == 1, (cut >> 6) & 63, cut >> 12))
    digits = digits.astype(jnp.float32).astype(jnp.bfloat16)
    repeated(o_ref, 0, q_ref[...])
    repeated(o_ref, WIDTH, digits)


def pack(queries, cutoffs, receivers):
    rows = queries.shape[0]
    return pl.pallas_call(
        pack_kernel,
        in_specs=[
            pl.BlockSpec(memory_space=pltpu.VMEM),
            pl.BlockSpec(memory_space=pltpu.SMEM),
        ],
        out_shape=jax.ShapeDtypeStruct((receivers * rows, PACKED), jnp.bfloat16),
        name="pack",
    )(queries, cutoffs)


def combine_kernel(p_ref, o_ref):
    rows = 8
    sources = p_ref.shape[0] // rows
    levels = []
    for n in range(sources // 2):
        level = level_of(p_ref[2 * n * rows : 2 * (n + 1) * rows, WIDTH:])
        levels += [level[:rows], level[rows:]]
    top = functools.reduce(jnp.maximum, levels)
    shares = [jnp.exp2(level - top) for level in levels]
    total = 1.0 / functools.reduce(jnp.add, shares)
    shares = [share * total for share in shares]
    sums = [jnp.zeros((rows, HEAD_DIM), jnp.float32) for _ in range(GROUP)]
    for n in range(sources // 2):
        for h in range(GROUP):
            part = p_ref[2 * n * rows : 2 * (n + 1) * rows, h * HEAD_DIM : (h + 1) * HEAD_DIM]
            part = part.astype(jnp.float32)
            sums[h] = sums[h] + part[:rows] * shares[2 * n][:, h : h + 1]
            sums[h] = sums[h] + part[rows:] * shares[2 * n + 1][:, h : h + 1]
    for h in range(GROUP):
        repeated(o_ref, h * HEAD_DIM, sums[h].astype(jnp.bfloat16))


def combine(parts, receivers):
    return pl.pallas_call(
        combine_kernel,
        out_shape=jax.ShapeDtypeStruct((8 * receivers, WIDTH), jnp.bfloat16),
        compiler_params=pltpu.CompilerParams(vmem_limit_bytes=SMALL),
        name="combine",
    )(parts)


def project_kernel(a_ref, w_ref, w_core, w_chip, w_both, o_ref):
    half = a_ref.shape[0] // 2
    chip = lax.axis_index("zl")
    core = lax.axis_index("c")
    attended = a_ref[...]
    for there, that, weight in (
        (chip, core, w_ref),
        (chip, 1 - core, w_core),
        (1 - chip, core, w_chip),
        (1 - chip, 1 - core, w_both),
    ):
        part = jnp.dot(attended, weight[...], preferred_element_type=jnp.float32)
        for y in range(half // 8):
            pair = [part[8 * y : 8 * y + 8], part[half + 8 * y : half + 8 * y + 8]]
            at = pl.multiple_of(((y % 4 * 2 + y // 4) * 4 + there * 2 + that) * 16, 16)
            o_ref[pl.ds(at, 16), :] = jnp.concatenate(pair, axis=0).astype(o_ref.dtype)


def project(attended, *weights):
    rows = attended.shape[0]
    return pl.pallas_call(
        project_kernel,
        out_shape=jax.ShapeDtypeStruct((len(weights) * rows, LANES), jnp.bfloat16),
        compiler_params=pltpu.CompilerParams(vmem_limit_bytes=SMALL),
        name="project",
    )(attended, *weights)


def total_kernel(s_ref, o_ref):
    near, heads, rows = 4, 8, 16
    half = rows // 2
    for n in range(near):
        parts = [
            s_ref[(h * near + n) * rows : (h * near + n + 1) * rows, :].astype(jnp.float32)
            for h in range(heads)
        ]
        total = functools.reduce(jnp.add, parts)
        for z in range(2):
            at = (z * near + n) * half
            o_ref[at : at + half, :] = total[z * half : (z + 1) * half]


def total_of(sums):
    return pl.pallas_call(
        total_kernel,
        out_shape=jax.ShapeDtypeStruct((64, LANES), jnp.float32),
        compiler_params=pltpu.CompilerParams(vmem_limit_bytes=SMALL),
        name="total",
    )(sums)


def exchange(x, axis):
    return lax.all_to_all(x, axis, 0, 0, tiled=True)


def shards(queries, keys, values, cutoffs, out_weight):
    far = SIZES[0] * SIZES[1] * SIZES[2] * SIZES[3]
    k_other = lax.ppermute(keys, "c", SWAP)
    v_other = lax.ppermute(values, "c", SWAP)
    packed = exchange(pack(queries, cutoffs, 2 * far), QUERIES)
    pairs = (keys, values, k_other, v_other)
    away = lax.ppermute(attend(packed, 1, *pairs), "zl", SWAP)
    parts = exchange(merge(attend(packed, 0, *pairs), away), FAR)
    w_core = lax.ppermute(out_weight, "c", SWAP)
    w_chip = lax.ppermute(out_weight, "zl", SWAP)
    w_both = lax.ppermute(w_chip, "c", SWAP)
    attended = exchange(combine(parts, far), FAR)
    sums = project(attended, out_weight, w_core, w_chip, w_both)
    return total_of(exchange(sums, ("x", "w") + NEAR))


def solution(mesh):
    fine = Mesh(mesh.devices.reshape(SIZES), AXES)
    return jax.shard_map(
        shards,
        mesh=fine,
        in_specs=(P(BLK, HEAD), P(BLK, HEAD), P(BLK, HEAD), P(BLK), P(HEAD, BLK)),
        out_specs=P(HEAD, BLK),
        check_vma=False,
    )
```
